32 devices in a mesh: dp: 16 (over z, x, core), mp: 2 (over y).
Axes of the slice: x: 2, y: 2, z: 4, core: 2. Of those that a mesh axis runs over, the one named last changes fastest.
Arguments:
- latents: bfloat16 [8192, 1152], P(('dp', 'mp')), may hold values from -6 to 6
- timesteps: int32 [32], P(('dp', 'mp')), may hold values from 0 to 999, as said below
- rel_index: int32 [256, 256], replicated, may hold values from 0 to 960, as said below
- time_table: bfloat16 [1000, 1152], replicated, may hold values from -6 to 6
- rel_bias: bfloat16 [16, 961], replicated, may hold values from -6 to 6
- w_mod: bfloat16 [1152, 4608], replicated, may hold values from -0.09375 to 0.09375
- b_mod: bfloat16 [4608], replicated, may hold values from -4 to 4
- w_qkv: bfloat16 [1152, 3456], replicated, may hold values from -0.1875 to 0.1875
- w_time: bfloat16 [1152, 2304], replicated, may hold values from -0.09375 to 0.09375
- w_out: bfloat16 [1152, 1152], replicated, may hold values from -0.375 to 0.375
- b_out: bfloat16 [1152], replicated, may hold values from -4 to 4
- w_up: bfloat16 [1152, 4608], P(None, 'mp'), may hold values from -0.1875 to 0.1875
- b_up: bfloat16 [4608], P('mp'), may hold values from -6 to 6
- w_down: bfloat16 [4608, 1152], P('mp'), may hold values from -0.09375 to 0.09375
- b_down: bfloat16 [1152], replicated, may hold values from -4 to 4
- cotangent: bfloat16 [8192, 1152], P(('dp', 'mp')), may hold values from -6 to 6
Outputs:
- out: bfloat16 [8192, 1152], P(('dp', 'mp'))
- grad_latents: bfloat16 [8192, 1152], P(('dp', 'mp'))
- grad_time_table: float32 [1000, 1152], P(None, ('dp', 'mp'))
- grad_rel_bias: float32 [16, 961], replicated
- grad_w_mod: float32 [1152, 4608], P(('dp', 'mp'))
- grad_b_mod: float32 [4608], P(('dp', 'mp'))
- grad_w_qkv: float32 [1152, 3456], P(('dp', 'mp'))
- grad_w_time: float32 [1152, 2304], P(('dp', 'mp'))
- grad_w_out: float32 [1152, 1152], P(('dp', 'mp'))
- grad_b_out: float32 [1152], P(('dp', 'mp'))
- grad_w_up: float32 [1152, 4608], P('dp', 'mp')
- grad_b_up: float32 [4608], P('mp')
- grad_w_down: float32 [4608, 1152], P('mp', 'dp')
- grad_b_down: float32 [1152], P(('dp', 'mp'))
The draws below stay inside these ranges and needn't reach their ends.
Inputs may be any that keep to these rules, and one draw needn't show every extreme that they name: `timesteps`: some image has timestep 0 and some has timestep 1000 - 1. rel_index[s, t] depends only on the offsets of patch t from patch s along the two sides of the 16 x 16 grid, and different offsets have different entries.
All inputs are finite; a program needn't handle non-finite values.
Results may differ from the reference program's by a relative error of at most 0.015.
Values may be sent and summed in bfloat16 or wider, within the bound.
No kernel may reach another device: no remote copies, remote signals or barrier semaphores. Data moves between devices by JAX's collectives and lax.ppermute only.
A program may use at most 320 MiB of HBM per device.

```python
from functools import partial
import jax
import jax.numpy as jnp
from jax import lax

D = 1152
HEADS = 16
HEAD_DIM = 72
FF = 4608
TSTEPS = 1000
GRID = 16
SEQ = 256
NREL = 961
IMAGES = 32
TOKENS = 8192


def draw_timesteps(key, part):
    key_mid, key_tail, key_pick, key_top, key_bottom = jax.random.split(key, 5)
    middle = jax.random.randint(key_mid, (IMAGES,), TSTEPS * 2 // 5, TSTEPS * 3 // 5)
    tails = jax.random.randint(key_tail, (IMAGES,), 0, TSTEPS)
    picked = jax.random.randint(key_pick, (IMAGES,), 0, 10) < 7
    drawn = jnp.where(picked, middle, tails)
    highest = jax.random.randint(key_top, (), 0, IMAGES)
    lowest = (highest + jax.random.randint(key_bottom, (), 1, IMAGES)) % IMAGES
    places = jnp.arange(IMAGES)
    drawn = jnp.where(places == highest, TSTEPS - 1, drawn)
    drawn = jnp.where(places == lowest, 0, drawn)
    return drawn.astype(jnp.int32)


def draw_rel_index(key, part):
    order = jax.random.permutation(jax.random.fold_in(key, 7), NREL)
    places = jnp.arange(SEQ)
    along_row = places // GRID
    along_col = places % GRID
    offset = (along_row[:, None] - along_row[None, :] + GRID - 1) * (2 * GRID - 1) + (along_col[:, None] - along_col[None, :] + GRID - 1)
    return order[offset].astype(jnp.int32)


def strengthened(array, own_key, source, target, parts, factor):
    def block_of(axis_at):
        return (jnp.arange(array.shape[axis_at]) // (array.shape[axis_at] // parts)).reshape((-1,) + (1,) * (array.ndim - 1 - axis_at))

    first = jax.random.permutation(own_key, parts)[block_of(target)]
    far = (block_of(target) + parts // 2) % parts
    return jnp.where((block_of(source) == first) | (block_of(source) == far), factor * array, array)


def shard_levels(key, dims, pieces, least, high):
    def one(position, blocks):
        heights = jax.random.uniform(jax.random.fold_in(jax.random.fold_in(key, 6), position), (blocks,), jnp.float32, least / len(pieces), high / len(pieces))
        return jnp.repeat(jnp.exp(heights), dims[position] // blocks).reshape((-1,) + (1,) * (len(dims) - position - 1))

    loudness = one(*pieces[0])
    for cut in pieces[1:]:
        loudness = loudness * one(*cut)
    return loudness


def gaussian(key, shape, scale, bound, cuts=(), dtype=jnp.bfloat16):
    level = shard_levels(key, shape, cuts, -0.22, 0.18) if cuts else 1.0
    array = jax.random.normal(key, shape, jnp.float32) * scale * level
    return jnp.minimum(jnp.maximum(array, -bound), bound).astype(dtype)


def bell_draw_with(stream_key, shape, spread, bound, pieces, heavy, dtype=jnp.bfloat16):
    values = spread * jax.random.normal(stream_key, shape, jnp.float32)
    if pieces:
        values = values * shard_levels(stream_key, shape, pieces, -0.22, 0.18)
    return jnp.clip(strengthened(values, jax.random.fold_in(stream_key, 3), *heavy), -bound, bound).astype(dtype)


def setup_inputs(seed: int = 0) -> dict:
    key_of = jax.random.split(jax.random.key(seed), 17)
    return {
        "latents": gaussian(key_of[0], (TOKENS, D), 1.0, 6.0, ((0, 32),)),
        "timesteps": draw_timesteps(jax.random.fold_in(key_of[16], 71), 0),
        "rel_index": draw_rel_index(jax.random.fold_in(key_of[16], 71), 0),
        "time_table": gaussian(key_of[3], (TSTEPS, D), 1.0, 6.0),
        "rel_bias": gaussian(key_of[4], (HEADS, NREL), 1.0, 6.0),
        "w_mod": gaussian(key_of[5], (D, 4 * D), (4 * D) ** -0.5, 0.09375),
        "b_mod": gaussian(key_of[6], (4 * D,), 0.3, 4.0),
        "w_qkv": gaussian(key_of[7], (D, 3 * D), D ** -0.5, 0.1875),
        "w_time": gaussian(key_of[8], (D, 2 * D), (4 * D) ** -0.5, 0.09375),
        "w_out": gaussian(key_of[9], (D, D), (D // 4) ** -0.5, 0.375),
        "b_out": gaussian(key_of[10], (D,), 0.3, 4.0),
        "w_up": gaussian(key_of[11], (D, FF), D ** -0.5, 0.1875, ((1, 2),)),
        "b_up": gaussian(key_of[12], (FF,), 0.5, 6.0, ((0, 2),)),
        "w_down": gaussian(key_of[13], (FF, D), FF ** -0.5, 0.09375, ((0, 2),)),
        "b_down": gaussian(key_of[14], (D,), 0.3, 4.0),
        "cotangent": bell_draw_with(key_of[15], (TOKENS, D), 1.0, 6.0, ((0, 32),), (0, 1, 32, 2.75)),
    }


EPSILON = 1e-06

@jax.custom_vjp
def low(v):
    return lax.optimization_barrier(v.astype(jnp.bfloat16)).astype(jnp.float32)

@jax.custom_vjp
def low_back(v):
    return v

def low_keep(v):
    return (low(v), None)

def low_pass(kept, grad):
    return (grad,)

def back_keep(v):
    return (v, None)

def back_low(kept, grad):
    return (low(grad),)
low.defvjp(low_keep, low_pass)
low_back.defvjp(back_keep, back_low)

def dot_high(first_op, second_op):
    return jnp.dot(first_op, second_op, precision=lax.Precision.HIGHEST)

def normalize(values):
    center = values - lax.optimization_barrier(jnp.mean(values, axis=-1, keepdims=True))
    return center * lax.rsqrt(lax.optimization_barrier(jnp.mean(center * center, axis=-1, keepdims=True)) + EPSILON)

def attend_one(operands, bias_table):
    query_rows, key_rows, value_rows = operands
    query_heads = query_rows.reshape(SEQ, HEADS, HEAD_DIM)
    key_heads = key_rows.reshape(SEQ, HEADS, HEAD_DIM)
    value_heads = value_rows.reshape(SEQ, HEADS, HEAD_DIM)
    scores = HEAD_DIM ** (-0.5) * jnp.einsum('shd,thd->hst', query_heads, key_heads, precision=lax.Precision.HIGHEST) + bias_table
    scores = low_back(scores)
    weights = low(jax.nn.softmax(scores, axis=-1))
    mixture = jnp.einsum('hst,thd->shd', weights, value_heads, precision=lax.Precision.HIGHEST)
    return mixture.reshape(SEQ, D)

def block_forward(inputs, step_ids, rel_index, time_table, rel_bias, w_mod, b_mod, w_qkv, w_time, w_out, b_out, w_up, b_up, w_down, b_down):
    embedding = time_table[step_ids]
    modulation = low_back(dot_high(low(jax.nn.silu(embedding)), w_mod) + b_mod)
    time_terms = low_back(dot_high(embedding, w_time))
    shift_one = modulation[:, None, 0:D]
    scale_one = modulation[:, None, D:2 * D]
    shift_two = modulation[:, None, 2 * D:3 * D]
    scale_two = modulation[:, None, 3 * D:4 * D]
    attn_in = low(normalize(inputs) * (1.0 + scale_one) + shift_one)
    projected = jnp.einsum('gsd,de->gse', attn_in, w_qkv, precision=lax.Precision.HIGHEST)
    queries = low(low_back(projected[..., 0:D] + time_terms[:, None, 0:D]))
    key_rows = low(low_back(projected[..., D:2 * D]))
    values = low(low_back(projected[..., 2 * D:3 * D] + time_terms[:, None, D:2 * D]))
    bias_table = rel_bias[:, rel_index]
    attended = lax.map(jax.checkpoint(partial(attend_one, bias_table=bias_table)), (queries, key_rows, values))
    attended = low(low_back(attended))
    branch = jnp.einsum('gsd,de->gse', attended, w_out, precision=lax.Precision.HIGHEST) + b_out
    middle = inputs + low_back(branch)
    mlp_in = low(normalize(middle) * (1.0 + scale_two) + shift_two)
    pre_act = low_back(jnp.einsum('gsd,df->gsf', mlp_in, w_up, precision=lax.Precision.HIGHEST) + b_up)
    activated = low(jax.nn.gelu(pre_act, approximate=False))
    return middle + jnp.einsum('gsf,fd->gsd', activated, w_down, precision=lax.Precision.HIGHEST) + b_down

def reference(latents, timesteps, rel_index, time_table, rel_bias, w_mod, b_mod, w_qkv, w_time, w_out, b_out, w_up, b_up, w_down, b_down, cotangent):
    params = tuple((tensor.astype(jnp.float32) for tensor in (time_table, rel_bias, w_mod, b_mod, w_qkv, w_time, w_out, b_out, w_up, b_up, w_down, b_down)))
    group_size = 16 if IMAGES % 16 == 0 else IMAGES
    group_count = IMAGES // group_size
    latent_groups = latents.astype(jnp.float32).reshape(group_count, group_size, SEQ, D)
    cotangent_groups = cotangent.astype(jnp.float32).reshape(group_count, group_size, SEQ, D)
    step_groups = timesteps.reshape(group_count, group_size)

    def one_group(totals, operands):
        inputs, cotangents, step_ids = operands

        def forward(inputs, *weights):
            return block_forward(inputs, step_ids, rel_index, *weights)
        result, pullback = jax.vjp(forward, inputs, *params)
        gradients = pullback(cotangents)
        updated = tuple((running + adding for running, adding in zip(totals, gradients[1:])))
        return (updated, (result, gradients[0]))
    initial = tuple((jnp.zeros_like(tensor) for tensor in params))
    totals, (results, grad_inputs) = lax.scan(one_group, initial, (latent_groups, cotangent_groups, step_groups))
    out = results.reshape(TOKENS, D).astype(jnp.bfloat16)
    grad_latents = grad_inputs.reshape(TOKENS, D).astype(jnp.bfloat16)
    return (out, grad_latents, totals[0], totals[1], totals[2], totals[3], totals[4], totals[5], totals[6], totals[7], totals[8], totals[9], totals[10], totals[11])
```

```python
import math

import jax
import jax.numpy as jnp
import numpy as np
from jax import lax
from jax.experimental import pallas as pl
from jax.experimental.pallas import tpu as pltpu
from jax.sharding import PartitionSpec as P

EPSILON = 1e-06
F32 = jnp.float32
BF16 = jnp.bfloat16


def normalize(values):
    center = values - jnp.mean(values, axis=-1, keepdims=True)
    inverse = lax.rsqrt(jnp.mean(center * center, axis=-1, keepdims=True) + EPSILON)
    return (center * inverse, inverse)


def normalize_back(gradient, normed, inverse):
    return inverse * (
        gradient
        - jnp.mean(gradient, axis=-1, keepdims=True)
        - normed * jnp.mean(gradient * normed, axis=-1, keepdims=True)
    )


def times(first_op, second_op):
    return jnp.dot(first_op, second_op, preferred_element_type=F32)


def contract_rows(first_op, second_op):
    return lax.dot_general(
        first_op, second_op, (((0,), (0,)), ((), ())), preferred_element_type=F32
    )


def times_transpose(first_op, second_op):
    return lax.dot_general(
        first_op, second_op, (((1,), (1,)), ((), ())), preferred_element_type=F32
    )


def spread_bias(shifted, seq_len):
    head_count, grid, _ = shifted.shape

    def body(in_ref, out_ref):
        for i in range(grid):
            start = grid * (grid - 1 - i)
            out_ref[:, i * grid : (i + 1) * grid, :] = in_ref[:, :, start : start + seq_len]

    return pl.pallas_call(
        body,
        out_shape=jax.ShapeDtypeStruct((head_count, seq_len, seq_len), F32),
        name="spread_bias",
    )(shifted)


def gather_bias(score_grads, grid):
    head_count, seq_len, _ = score_grads.shape

    def body(in_ref, out_ref):
        total = jnp.zeros((head_count, grid, 2 * seq_len), F32)
        blank = jnp.zeros((head_count, grid, seq_len), F32)
        for i in range(grid):
            start = grid * (grid - 1 - i)
            rows = in_ref[:, i * grid : (i + 1) * grid, :].astype(F32)
            wide = jnp.concatenate([rows, blank], axis=-1)
            wide = wide.reshape(head_count * grid, 2 * seq_len)
            wide = pltpu.roll(wide, start, 1) if start else wide
            total = total + wide.reshape(head_count, grid, 2 * seq_len)
        out_ref[...] = total

    return pl.pallas_call(
        body,
        out_shape=jax.ShapeDtypeStruct((head_count, grid, 2 * seq_len), F32),
        name="gather_bias",
    )(score_grads)


def relative_blocks(bits, count):
    depth = len(bits)
    table = np.zeros((count,), np.int32)
    for place in range(count):
        for k, bit in enumerate(bits):
            table[place] |= ((place >> (depth - 1 - k)) & 1) << bit
    return table


def select_columns(blocks, mine, width):
    count = blocks.shape[0]
    size = width // count
    base = np.repeat(blocks, size)
    offset = np.tile(np.arange(size, dtype=np.int32), count)
    source = (jnp.asarray(base) ^ mine) * size + jnp.asarray(offset)
    rows = lax.broadcasted_iota(jnp.int32, (width, width), 0)
    return (rows == source[None, :]).astype(BF16)


def make_device(mesh):
    dp_size = mesh.shape["dp"]
    mp_size = mesh.shape["mp"]
    all_size = dp_size * mp_size
    dp_bits = dp_size.bit_length() - 1

    def swap(values, bit):
        if bit == 0:
            return lax.ppermute(values, "mp", [(i, i ^ 1) for i in range(mp_size)])
        return lax.ppermute(
            values, "dp", [(i, i ^ (1 << (bit - 1))) for i in range(dp_size)]
        )

    dp_order = list(range(1, dp_bits + 1))
    all_order = [1, 0] + list(range(2, dp_bits + 1))

    def scatter_sum(turned, other, order):
        total = turned.shape[0]

        def part(low, high, received):
            value = times(turned[low:high], other)
            for item in received:
                value = value + item[low:high].astype(F32)
            return value

        received = []
        high = total
        for bit in order:
            low = high // 2
            received.append(swap(part(low, high, received).astype(BF16), bit))
            high = low
        return part(0, high, received)

    def on_device(
        latents,
        timesteps,
        rel_index,
        time_table,
        rel_bias,
        w_mod,
        b_mod,
        w_qkv,
        w_time,
        w_out,
        b_out,
        w_up,
        b_up,
        w_down,
        b_down,
        cotangent,
    ):
        seq_len, model_width = latents.shape
        head_count, entries = rel_bias.shape
        head_size = model_width // head_count
        score_scale = head_size ** (-0.5)
        grid = math.isqrt(seq_len)
        span = 2 * grid - 1
        table_size = time_table.shape[0]
        dp_at = lax.axis_index("dp")
        mp_at = lax.axis_index("mp")
        device = dp_at * mp_size + mp_at

        peer_cotangent = swap(cotangent, 0)

        dp_blocks = relative_blocks([b - 1 for b in dp_order], dp_size)
        all_blocks = relative_blocks(all_order, all_size)
        dp_select = select_columns(dp_blocks, dp_at, model_width)
        all_select = select_columns(all_blocks, device, model_width)

        step = timesteps[0]
        embedding = lax.dynamic_slice(time_table, (step, 0), (1, model_width))
        embed_float = embedding.astype(F32)
        silu_low = jax.nn.silu(embed_float).astype(BF16)
        modulation = times(silu_low, w_mod) + b_mod.astype(F32)
        shift_one = modulation[:, 0:model_width]
        scale_one = modulation[:, model_width : 2 * model_width]
        shift_two = modulation[:, 2 * model_width : 3 * model_width]
        scale_two = modulation[:, 3 * model_width : 4 * model_width]
        time_terms = times(embedding, w_time)

        last = grid - 1
        index_grid = rel_index.reshape(grid, grid, grid, grid)
        upper = jnp.concatenate(
            [index_grid[last, last, :last, :last], index_grid[last, 0, :last, :]], axis=1
        )
        lower = jnp.concatenate(
            [index_grid[0, last, :, :last], index_grid[0, 0, :, :]], axis=1
        )
        entry_of = jnp.concatenate([upper, lower], axis=0).reshape(-1)
        places = lax.broadcasted_iota(jnp.int32, (entries, span * span), 0)
        entry_select = (places == entry_of[None, :]).astype(BF16)
        by_offset = times(rel_bias, entry_select).reshape(head_count, span, span)
        shifted = jnp.stack(
            [by_offset[:, :, last - j : last - j + grid] for j in range(grid)], axis=1
        ).reshape(head_count, grid, span * grid)
        shifted = jnp.pad(shifted, ((0, 0), (0, 0), (0, 2 * seq_len - span * grid)))
        bias_table = spread_bias(shifted, seq_len)

        inputs = latents.astype(F32)
        normed_one, inverse_one = normalize(inputs)
        attn_in = (normed_one * (1.0 + scale_one) + shift_one).astype(BF16)
        projected = times(attn_in, w_qkv)
        queries = (projected[:, 0:model_width] + time_terms[:, 0:model_width]).astype(BF16)
        key_rows = projected[:, model_width : 2 * model_width].astype(BF16)
        values = (projected[:, 2 * model_width :] + time_terms[:, model_width:]).astype(BF16)

        def heads_of(rows):
            return rows.reshape(seq_len, head_count, head_size)

        def einsum(form, first_op, second_op):
            return jnp.einsum(form, first_op, second_op, preferred_element_type=F32)

        query_heads, key_heads, value_heads = (
            heads_of(queries),
            heads_of(key_rows),
            heads_of(values),
        )

        def scores_of():
            return score_scale * einsum("shd,thd->hst", query_heads, key_heads) + bias_table

        scores = scores_of()
        row_max = jnp.max(scores, axis=-1, keepdims=True)
        exponent = jnp.exp(scores - row_max)
        row_total = jnp.sum(exponent, axis=-1, keepdims=True)
        attn_low = (exponent / row_total).astype(BF16)
        attended = einsum("hst,thd->shd", attn_low, value_heads)
        attended = attended.reshape(seq_len, model_width).astype(BF16)
        log_total = row_max + jnp.log(row_total)

        middle = inputs + (times(attended, w_out) + b_out.astype(F32))
        normed_two, inverse_two = normalize(middle)
        mlp_in = (normed_two * (1.0 + scale_two) + shift_two).astype(BF16)
        peer_in = swap(mlp_in, 0)

        bias_up = b_up.astype(F32)

        def hidden(rows, grads):
            pre_act = times(rows, w_up) + bias_up
            below = 0.5 * (1.0 + lax.erf(pre_act * math.sqrt(0.5)))
            slope = below + pre_act * (
                jnp.exp(-0.5 * pre_act * pre_act) * (1.0 / math.sqrt(2.0 * math.pi))
            )
            grad_pre = slope * times_transpose(grads, w_down)
            return (pre_act * below).astype(BF16), grad_pre.astype(BF16)

        own_act, own_grad_pre = hidden(mlp_in, cotangent)
        own_back = times_transpose(own_grad_pre, w_up)
        own_out = times(own_act, w_down)
        peer_act, peer_grad_pre = hidden(peer_in, peer_cotangent)
        back_received = swap(times_transpose(peer_grad_pre, w_up).astype(BF16), 0)
        out_received = swap(times(peer_act, w_down).astype(BF16), 0)

        out = (
            middle + (own_out + out_received.astype(F32)) + b_down.astype(F32)
        ).astype(BF16)

        both_act = jnp.concatenate([own_act, peer_act], axis=0)
        both_grad_pre = jnp.concatenate([own_grad_pre, peer_grad_pre], axis=0)
        both_in = jnp.concatenate([mlp_in, peer_in], axis=0)
        both_cotangent = jnp.concatenate([cotangent, peer_cotangent], axis=0)

        def turned(select, rows):
            return lax.dot_general(
                select, rows, (((0,), (1,)), ((), ())), preferred_element_type=F32
            ).astype(BF16)

        grad_w_down = scatter_sum(turned(dp_select, both_cotangent), both_act, dp_order).T
        grad_w_up = scatter_sum(turned(dp_select, both_in), both_grad_pre, dp_order)

        grad_mlp_in = own_back + back_received.astype(F32)
        grad_shift_two = jnp.sum(grad_mlp_in, axis=0)
        grad_scale_two = jnp.sum(grad_mlp_in * normed_two, axis=0)
        grad_middle = cotangent.astype(F32) + normalize_back(
            grad_mlp_in * (1.0 + scale_two), normed_two, inverse_two
        )
        grad_branch = grad_middle.astype(BF16)
        grad_attended = times_transpose(grad_branch, w_out).astype(BF16)
        grad_w_out = scatter_sum(turned(all_select, attended), grad_branch, all_order)

        grad_heads = heads_of(grad_attended)
        attention = jnp.exp(scores_of() - log_total)
        attn_low = attention.astype(BF16)
        grad_attn = einsum("shd,thd->hst", grad_heads, value_heads)
        grad_scores = (
            attention * (grad_attn - jnp.sum(attention * grad_attn, axis=-1, keepdims=True))
        ).astype(BF16)
        grad_query = score_scale * einsum("hst,thd->shd", grad_scores, key_heads)
        grad_key = score_scale * einsum("hst,shd->thd", grad_scores, query_heads)
        grad_value = einsum("hst,shd->thd", attn_low, grad_heads)
        grad_projected = jnp.concatenate(
            [
                grad_query.reshape(seq_len, model_width),
                grad_key.reshape(seq_len, model_width),
                grad_value.reshape(seq_len, model_width),
            ],
            axis=1,
        ).astype(BF16)
        grad_w_qkv = scatter_sum(turned(all_select, attn_in), grad_projected, all_order)
        grad_attn_in = times_transpose(grad_projected, w_qkv)
        grad_time = jnp.concatenate(
            [
                jnp.sum(grad_projected[:, 0:model_width].astype(F32), axis=0),
                jnp.sum(grad_projected[:, 2 * model_width :].astype(F32), axis=0),
            ]
        ).astype(BF16)

        wide = gather_bias(grad_scores, grid)[:, :, : span * grid]
        wide = wide.reshape(head_count, grid, span, grid)
        grad_by_offset = sum(
            jnp.pad(wide[:, j], ((0, 0), (0, 0), (last - j, j))) for j in range(grid)
        ).reshape(head_count, span * span)

        hidden_count = b_up.shape[0]
        grad_b_up_part = jnp.sum(both_grad_pre.astype(F32), axis=0)
        slots = jnp.where(
            lax.broadcasted_iota(jnp.int32, (mp_size, hidden_count), 0) == mp_at,
            grad_b_up_part[None, :],
            0.0,
        ).reshape(-1)
        packed = jnp.concatenate(
            [
                slots,
                jnp.sum(grad_branch.astype(F32), axis=0),
                jnp.sum(cotangent.astype(F32), axis=0),
                grad_by_offset.reshape(-1),
            ]
        )
        packed_size = packed.shape[0]
        rows = -(-packed_size // 1024) * 8
        packed = jnp.pad(packed, (0, rows * 128 - packed_size)).reshape(rows, 128)
        for bit in all_order:
            packed = packed + swap(packed, bit)
        packed = packed.reshape(-1)
        at = mp_size * hidden_count
        grad_b_up = lax.dynamic_slice(packed, (mp_at * hidden_count,), (hidden_count,))
        share = model_width // all_size
        grad_b_out = lax.dynamic_slice(packed, (at + device * share,), (share,))
        grad_b_down = lax.dynamic_slice(packed, (at + model_width + device * share,), (share,))
        at = at + 2 * model_width
        grad_by_offset = packed[at : at + head_count * span * span].reshape(head_count, -1)
        grad_rel_bias = lax.dot_general(
            grad_by_offset,
            entry_select.astype(F32),
            (((1,), (1,)), ((), ())),
            precision=lax.Precision.HIGHEST,
            preferred_element_type=F32,
        )

        grad_shift_one = jnp.sum(grad_attn_in, axis=0)
        grad_scale_one = jnp.sum(grad_attn_in * normed_one, axis=0)
        grad_latents = (
            grad_middle + normalize_back(grad_attn_in * (1.0 + scale_one), normed_one, inverse_one)
        ).astype(BF16)

        step_parts = jnp.zeros((128,), F32).at[0].set((step // 32).astype(F32))
        step_parts = step_parts.at[1].set((step % 32).astype(F32))
        image_row = jnp.concatenate(
            [
                grad_shift_one.astype(BF16),
                grad_scale_one.astype(BF16),
                grad_shift_two.astype(BF16),
                grad_scale_two.astype(BF16),
                grad_time,
                step_parts.astype(BF16),
            ]
        )[None, :]
        for bit in all_order[::-1]:
            image_row = jnp.concatenate([image_row, swap(image_row, bit)], axis=0)
        all_mod = image_row[:, : 4 * model_width]
        all_time = image_row[:, 4 * model_width : 6 * model_width]
        parts = image_row[:, 6 * model_width :].astype(F32)
        all_steps = (parts[:, 0] * 32.0 + parts[:, 1]).astype(jnp.int32)
        step_select = (
            all_steps[:, None] == lax.broadcasted_iota(jnp.int32, (all_size, table_size), 1)
        )
        own_table = times(time_table, all_select[:, :share]).astype(BF16)
        own_embed = times(step_select.astype(BF16), own_table).astype(BF16)
        own_float = own_embed.astype(F32)
        own_silu, silu_pull = jax.vjp(jax.nn.silu, own_float)
        grad_w_mod = contract_rows(own_silu.astype(BF16), all_mod)
        grad_w_time = contract_rows(own_embed, all_time)
        mod_share = 4 * model_width // all_size
        grad_b_mod = lax.dynamic_slice(
            jnp.sum(all_mod.astype(F32), axis=0), (device * mod_share,), (mod_share,)
        )
        own_w_mod = lax.dynamic_slice(w_mod, (device * share, 0), (share, 4 * model_width))
        own_w_time = lax.dynamic_slice(w_time, (device * share, 0), (share, 2 * model_width))
        grad_embed = silu_pull(times_transpose(all_mod, own_w_mod))[0] + times_transpose(
            all_time, own_w_time
        )
        grad_table = lax.dot_general(
            step_select.astype(F32),
            grad_embed,
            (((0,), (0,)), ((), ())),
            precision=lax.Precision.HIGHEST,
            preferred_element_type=F32,
        )
        return (
            out,
            grad_latents,
            grad_table,
            grad_rel_bias,
            grad_w_mod,
            grad_b_mod,
            grad_w_qkv,
            grad_w_time,
            grad_w_out,
            grad_b_out,
            grad_w_up,
            grad_b_up,
            grad_w_down,
            grad_b_down,
        )

    return on_device


def solution(mesh):
    both = ("dp", "mp")
    in_specs = (
        P(both, None),
        P(both),
        P(),
        P(),
        P(),
        P(),
        P(),
        P(),
        P(),
        P(),
        P(),
        P(None, "mp"),
        P("mp"),
        P("mp", None),
        P(),
        P(both, None),
    )
    out_specs = (
        P(both, None),
        P(both, None),
        P(None, both),
        P(),
        P(both, None),
        P(both),
        P(both, None),
        P(both, None),
        P(both, None),
        P(both),
        P("dp", "mp"),
        P("mp"),
        P("mp", "dp"),
        P(both),
    )
    return jax.shard_map(
        make_device(mesh), mesh=mesh, in_specs=in_specs, out_specs=out_specs, check_vma=False
    )
```

```python
import functools
import math

import jax
import jax.numpy as jnp
import numpy as np
from jax import lax
from jax.experimental import pallas as pl
from jax.experimental.pallas import tpu as pltpu
from jax.sharding import PartitionSpec as P

EPSILON = 1e-06
F32 = jnp.float32
BF16 = jnp.bfloat16
ANY = pl.BlockSpec(memory_space=pl.ANY)
VMEM = pl.BlockSpec(memory_space=pltpu.VMEM)
SMEM = pl.BlockSpec(memory_space=pltpu.SMEM)
ROWS = 32
LINE = 256


def times(first_op, second_op):
    return jnp.dot(first_op, second_op, preferred_element_type=F32)


def contract_rows(first_op, second_op):
    return lax.dot_general(
        first_op, second_op, (((0,), (0,)), ((), ())), preferred_element_type=F32
    )


def times_transpose(first_op, second_op):
    return lax.dot_general(
        first_op, second_op, (((1,), (1,)), ((), ())), preferred_element_type=F32
    )


def kernel_call(body, name, out_shape, in_specs, out_specs, scratch, after=()):
    count = len(in_specs)
    extra = len(after)

    def run(*refs):
        body(*refs[:count], *refs[count + extra :])

    call = pl.pallas_call(
        run,
        name=name,
        out_shape=out_shape,
        in_specs=list(in_specs) + [ANY] * extra,
        out_specs=out_specs,
        scratch_shapes=scratch,
        compiler_params=pltpu.CompilerParams(vmem_limit_bytes=56 * 2**20),
        cost_estimate=pl.CostEstimate(flops=1000, bytes_accessed=1000, transcendentals=0),
    )
    return lambda *operands: call(*operands, *after)


def shape(dims, dtype):
    return jax.ShapeDtypeStruct(dims, dtype)


class Copies:
    def __init__(self, sems):
        self.sems = sems
        self.count = 0

    def start(self, source, target):
        copy = pltpu.make_async_copy(source, target, self.sems.at[self.count])
        self.count += 1
        copy.start()
        return copy


def normalized(rows):
    center = rows - jnp.mean(rows, axis=-1, keepdims=True)
    inverse = lax.rsqrt(jnp.mean(center * center, axis=-1, keepdims=True) + EPSILON)
    return center * inverse, inverse


def back_normalized(gradient, normed, inverse):
    return inverse * (
        gradient
        - jnp.mean(gradient, axis=-1, keepdims=True)
        - normed * jnp.mean(gradient * normed, axis=-1, keepdims=True)
    )


def turn_into(target_ref, first_column, source_row_ref, rows_ref, step=384):
    count, width = rows_ref.shape
    for at in range(0, width, step):
        places = lax.broadcasted_iota(jnp.int32, (width, step), 0)
        select = (places == source_row_ref[:, at : at + step]).astype(BF16)
        picked = times(rows_ref[...], select)
        target_ref[at : at + step, first_column : first_column + count] = picked.T.astype(BF16)


def head_window(head, head_size):
    low = head * head_size
    start = low // 128 * 128
    stop = -(-(low + head_size) // 128) * 128
    lanes = lax.broadcasted_iota(jnp.int32, (1, stop - start), 1) + start
    inside = jnp.logical_and(lanes >= low, lanes < low + head_size)
    return start, stop, inside


def corner_rows(rel_index_ref, grid):
    last = grid - 1
    for place in (last * grid, grid * grid - 1, 0, last):
        yield rel_index_ref[place : place + 1, :]


def entry_select(rel_index_ref, entries, grid):
    places = lax.broadcasted_iota(jnp.int32, (entries, grid * grid), 0)
    return [(places == row).astype(BF16) for row in corner_rows(rel_index_ref, grid)]


def head_bias(corners, head, grid):
    seq = grid * grid
    shape_ = (grid, seq)
    lanes = lax.broadcasted_iota(jnp.int32, shape_, 1)
    rows = lax.broadcasted_iota(jnp.int32, shape_, 0)
    later = lanes % grid >= rows

    def moved(corner, shift):
        wide = jnp.broadcast_to(corner[head : head + 1, :], shape_)
        return pltpu.roll(wide, shift, 1, stride=1, stride_axis=0)

    first = jnp.where(later, moved(corners[0], 0), moved(corners[1], seq - grid + 1))
    second = jnp.where(later, moved(corners[2], 0), moved(corners[3], seq - grid + 1))
    edge = (grid - 1) * grid
    blank = jnp.zeros(shape_, F32)
    wide = jnp.where(
        lax.broadcasted_iota(jnp.int32, (grid, 2 * seq), 1) < edge,
        jnp.concatenate([first, blank], axis=1),
        pltpu.roll(jnp.concatenate([second, blank], axis=1), edge, 1),
    )
    parts = [
        wide[:, grid * (grid - 1 - i) : grid * (grid - 1 - i) + seq] for i in range(grid)
    ]
    return jnp.concatenate(parts, axis=0)


def head_bias_back(score_grads, grid):
    seq = grid * grid
    edge = (grid - 1) * grid
    wide = jnp.zeros((grid, 2 * seq), F32)
    blank = jnp.zeros((grid, seq), F32)
    for i in range(grid):
        start = grid * (grid - 1 - i)
        rows = jnp.concatenate([score_grads[i * grid : (i + 1) * grid, :], blank], axis=1)
        wide = wide + (pltpu.roll(rows, start, 1) if start else rows)
    shape_ = (grid, seq)
    lanes = lax.broadcasted_iota(jnp.int32, shape_, 1)
    places = lax.broadcasted_iota(jnp.int32, shape_, 0)
    later = lanes % grid >= places
    first = jnp.where(lanes < edge, wide[:, :seq], 0.0)
    second = pltpu.roll(wide, 2 * seq - edge, 1)[:, :seq]

    def moved(values, shift):
        bit = 1
        while bit < grid:
            values = jnp.where(places & bit > 0, pltpu.roll(values, seq - bit, 1), values)
            bit *= 2
        total = jnp.sum(values, axis=0, keepdims=True)
        return pltpu.roll(total, shift, 1) if shift else total

    return [
        moved(jnp.where(later, first, 0.0), 0),
        moved(jnp.where(later, 0.0, first), grid - 1),
        moved(jnp.where(later, second, 0.0), 0),
        moved(jnp.where(later, 0.0, second), grid - 1),
    ]


def front(
    latents, rel_index, rel_bias, embed, b_mod, w_mod, w_qkv, w_time, w_out, b_out, source_row
):
    seq, width = latents.shape
    heads, entries = rel_bias.shape
    size = width // heads
    grid = math.isqrt(seq)
    scale = size ** (-0.5)

    def body(
        latents_hbm,
        rel_index_ref,
        rel_bias_ref,
        embed_ref,
        b_mod_ref,
        w_mod_hbm,
        w_qkv_hbm,
        w_time_hbm,
        w_out_hbm,
        b_out_ref,
        source_ref,
        turned_keep_hbm,
        turned_send_hbm,
        qkv_hbm,
        probs_hbm,
        middle_hbm,
        mlp_in_hbm,
        mod_ref,
        latents_ref,
        w_mod_ref,
        w_qkv_ref,
        w_time_ref,
        w_out_ref,
        attn_in_ref,
        attn_turned_ref,
        attended_turned_ref,
        qkv_ref,
        probs_ref,
        total_ref,
        attended_ref,
        middle_ref,
        mlp_in_ref,
        sems,
    ):
        copies = Copies(sems)
        half = 2 * width
        get_latents = copies.start(latents_hbm, latents_ref)
        get_mod_one = copies.start(w_mod_hbm.at[:, :half], w_mod_ref.at[:, :half])
        get_time = copies.start(w_time_hbm, w_time_ref)
        get_qkv = [
            copies.start(
                w_qkv_hbm.at[:, k * width : (k + 1) * width],
                w_qkv_ref.at[:, k * width : (k + 1) * width],
            )
            for k in range(3)
        ]
        get_out = copies.start(w_out_hbm, w_out_ref)
        get_mod_two = copies.start(w_mod_hbm.at[:, half:], w_mod_ref.at[:, half:])
        puts = []

        corners = [
            times(rel_bias_ref[...], select)
            for select in entry_select(rel_index_ref, entries, grid)
        ]
        embed_rows = jnp.broadcast_to(embed_ref[...].astype(F32), (16, width))
        silu = (embed_rows / (1.0 + jnp.exp(-embed_rows))).astype(BF16)

        get_mod_one.wait()
        mod_ref[:, :half] = times(silu, w_mod_ref[:, :half])[0:8] + b_mod_ref[
            :, :half
        ].astype(F32)
        get_latents.wait()
        shift = mod_ref[0:1, 0:width]
        gain = 1.0 + mod_ref[0:1, width:half]
        for at in range(0, seq, ROWS):
            normed, _ = normalized(latents_ref[at : at + ROWS, :].astype(F32))
            attn_in_ref[at : at + ROWS, :] = (normed * gain + shift).astype(BF16)
        get_time.wait()
        time_terms = times(embed_rows.astype(BF16), w_time_ref[...])[0:1]
        extra = (time_terms[:, :width], None, time_terms[:, width:])
        for k in range(3):
            get_qkv[k].wait()
            for at in range(0, width, 384):
                low = k * width + at
                value = times(attn_in_ref[...], w_qkv_ref[:, low : low + 384])
                if extra[k] is not None:
                    value = value + extra[k][:, at : at + 384]
                qkv_ref[:, low : low + 384] = value.astype(BF16)
        puts.append(copies.start(qkv_ref, qkv_hbm))

        for head in range(heads):
            start, stop, inside = head_window(head, size)
            query = jnp.where(inside, qkv_ref[:, start:stop], jnp.zeros((), BF16))
            key = qkv_ref[:, width + start : width + stop]
            value = qkv_ref[:, 2 * width + start : 2 * width + stop]
            scores = times_transpose(query, key) * scale + head_bias(corners, head, grid)
            exponent = jnp.exp(scores - jnp.max(scores, axis=-1, keepdims=True))
            probs = exponent / jnp.sum(exponent, axis=-1, keepdims=True)
            probs = probs.astype(BF16)
            probs_ref[head] = probs
            mixture = times(probs, value)
            total_ref[:, start:stop] = jnp.where(inside, mixture, total_ref[:, start:stop])
        puts.append(copies.start(probs_ref, probs_hbm))
        attended_ref[...] = total_ref[...].astype(BF16)

        get_mod_two.wait()
        mod_ref[:, half:] = times(silu, w_mod_ref[:, half:])[0:8] + b_mod_ref[
            :, half:
        ].astype(F32)
        get_out.wait()
        total_ref[...] = times(attended_ref[...], w_out_ref[...])
        shift = mod_ref[0:1, half : half + width]
        gain = 1.0 + mod_ref[0:1, half + width :]
        bias = b_out_ref[...].astype(F32)
        for at in range(0, seq, ROWS):
            span = slice(at, at + ROWS)
            middle = latents_ref[span, :].astype(F32) + (total_ref[span, :] + bias)
            middle_ref[span, :] = middle
            normed, _ = normalized(middle)
            mlp_in_ref[span, :] = (normed * gain + shift).astype(BF16)
        puts.append(copies.start(mlp_in_ref, mlp_in_hbm))
        puts.append(copies.start(middle_ref, middle_hbm))
        rows = width // 2
        for k, (turned_ref, values_ref) in enumerate(
            ((attn_turned_ref, attn_in_ref), (attended_turned_ref, attended_ref))
        ):
            turn_into(turned_ref, 0, source_ref, values_ref)
            span = slice(k * rows, (k + 1) * rows)
            puts.append(copies.start(turned_ref.at[:rows], turned_keep_hbm.at[span]))
            puts.append(copies.start(turned_ref.at[rows:], turned_send_hbm.at[span]))
        for put in puts:
            put.wait()

    return kernel_call(
        body,
        "front",
        (
            shape((width, seq), BF16),
            shape((width, seq), BF16),
            shape((seq, 3 * width), BF16),
            shape((heads, seq, seq), BF16),
            shape((seq, width), F32),
            shape((seq, width), BF16),
            shape((8, 4 * width), F32),
        ),
        [ANY, VMEM, VMEM, VMEM, VMEM, ANY, ANY, ANY, ANY, VMEM, VMEM],
        (ANY, ANY, ANY, ANY, ANY, ANY, VMEM),
        [
            pltpu.VMEM((seq, width), BF16),
            pltpu.VMEM((width, 4 * width), BF16),
            pltpu.VMEM((width, 3 * width), BF16),
            pltpu.VMEM((width, 2 * width), BF16),
            pltpu.VMEM((width, width), BF16),
            pltpu.VMEM((seq, width), BF16),
            pltpu.VMEM((width, seq), BF16),
            pltpu.VMEM((width, seq), BF16),
            pltpu.VMEM((seq, 3 * width), BF16),
            pltpu.VMEM((heads, seq, seq), BF16),
            pltpu.VMEM((seq, width), F32),
            pltpu.VMEM((seq, width), BF16),
            pltpu.VMEM((seq, width), F32),
            pltpu.VMEM((seq, width), BF16),
            pltpu.SemaphoreType.DMA((16,)),
        ],
    )(
        latents,
        rel_index,
        rel_bias,
        embed,
        b_mod,
        w_mod,
        w_qkv,
        w_time,
        w_out,
        b_out,
        source_row,
    )


def feed_forward(rows, grads, w_up, b_up, w_down, source_row, own, after=()):
    seq, width = rows.shape
    hidden = w_up.shape[1]
    step = 256
    parts = 3
    chunk = hidden // parts

    def body(*refs):
        (rows_ref, grads_ref, w_up_hbm, b_up_ref, w_down_hbm, source_ref) = refs[:6]
        if own:
            (act_hbm, pre_hbm, back_hbm, sum_ref, out_hbm, rows_turned_hbm, grads_turned_hbm) = refs[6:13]
            scratch = refs[13:]
        else:
            (act_hbm, pre_hbm, back_hbm, sum_ref) = refs[6:10]
            scratch = refs[10:]
        (w_up_ref, w_down_ref, act_ref, pre_ref, back_ref, sems) = scratch[:6]
        copies = Copies(sems)
        gets = []
        for k in range(parts):
            span = slice(k * chunk, (k + 1) * chunk)
            gets.append(copies.start(w_up_hbm.at[:, span], w_up_ref.at[:, span]))
            gets.append(copies.start(w_down_hbm.at[span, :], w_down_ref.at[span, :]))
        puts = []
        if own:
            out_ref, rows_turned_ref, grads_turned_ref = scratch[6:9]
            turn_into(rows_turned_ref, 0, source_ref, rows_ref)
            puts.append(copies.start(rows_turned_ref, rows_turned_hbm))
            turn_into(grads_turned_ref, 0, source_ref, grads_ref)
            puts.append(copies.start(grads_turned_ref, grads_turned_hbm))
        for at in range(0, hidden, step):
            if at % chunk == 0:
                gets[2 * (at // chunk)].wait()
                gets[2 * (at // chunk) + 1].wait()
            span = slice(at, at + step)
            pre_act = times(rows_ref[...], w_up_ref[:, span]) + b_up_ref[:, span].astype(F32)
            grad_act = times_transpose(grads_ref[...], w_down_ref[span, :])
            below = 0.5 * (1.0 + lax.erf(pre_act * math.sqrt(0.5)))
            slope = below + pre_act * (
                jnp.exp(-0.5 * pre_act * pre_act) * (1.0 / math.sqrt(2.0 * math.pi))
            )
            act_ref[:, span] = (pre_act * below).astype(BF16)
            grad_pre = (slope * grad_act).astype(BF16)
            pre_ref[:, span] = grad_pre
            sum_ref[:, span] = jnp.sum(grad_pre.astype(F32), axis=0, keepdims=True)
        puts.append(copies.start(act_ref, act_hbm))
        puts.append(copies.start(pre_ref, pre_hbm))
        for at in range(0, width, 384):
            span = slice(at, at + 384)
            back_ref[:, span] = times_transpose(pre_ref[...], w_up_ref[span, :]).astype(
                back_ref.dtype
            )
        puts.append(copies.start(back_ref, back_hbm))
        if own:
            for at in range(0, width, 384):
                span = slice(at, at + 384)
                out_ref[:, span] = times(act_ref[...], w_down_ref[:, span])
            puts.append(copies.start(out_ref, out_hbm))
        for put in puts:
            put.wait()

    kind = F32 if own else BF16
    outs = [
        shape((seq, hidden), BF16),
        shape((seq, hidden), BF16),
        shape((seq, width), kind),
        shape((1, hidden), F32),
    ]
    specs = [ANY, ANY, ANY, VMEM]
    scratch = [
        pltpu.VMEM((width, hidden), BF16),
        pltpu.VMEM((hidden, width), BF16),
        pltpu.VMEM((seq, hidden), BF16),
        pltpu.VMEM((seq, hidden), BF16),
        pltpu.VMEM((seq, width), kind),
        pltpu.SemaphoreType.DMA((16,)),
    ]
    if own:
        outs += [shape((seq, width), F32), shape((width, seq), BF16), shape((width, seq), BF16)]
        specs += [ANY, ANY, ANY]
        scratch += [
            pltpu.VMEM((seq, width), F32),
            pltpu.VMEM((width, seq), BF16),
            pltpu.VMEM((width, seq), BF16),
        ]
    return kernel_call(
        body,
        "own_hidden" if own else "peer_hidden",
        tuple(outs),
        [VMEM, VMEM, ANY, VMEM, ANY, VMEM],
        tuple(specs),
        scratch,
        after,
    )(rows, grads, w_up, b_up, w_down, source_row)


def weight_products(
    rows, grads, source_row, rows_turned, grads_turned, own_act, peer_act, own_pre, peer_pre
):
    seq, width = rows.shape
    hidden = own_act.shape[1]
    half = width // 2
    parts = 3
    chunk = hidden // parts

    def body(
        rows_ref,
        grads_ref,
        source_ref,
        rows_turned_hbm,
        grads_turned_hbm,
        own_act_hbm,
        peer_act_hbm,
        own_pre_hbm,
        peer_pre_hbm,
        down_send_hbm,
        down_keep_hbm,
        up_send_hbm,
        up_keep_hbm,
        turned_ref,
        other_ref,
        send_ref,
        keep_ref,
        sems,
    ):
        copies = Copies(sems)
        gets = []
        for k, (turned, own, peer) in enumerate(
            (
                (grads_turned_hbm, own_act_hbm, peer_act_hbm),
                (rows_turned_hbm, own_pre_hbm, peer_pre_hbm),
            )
        ):
            gets.append(
                [
                    copies.start(turned, turned_ref.at[k, :, :seq]),
                    copies.start(own, other_ref.at[k, :seq, :]),
                    copies.start(peer, other_ref.at[k, seq:, :]),
                ]
            )
        puts = []
        turn_into(turned_ref.at[0], seq, source_ref, grads_ref)
        turn_into(turned_ref.at[1], seq, source_ref, rows_ref)
        for k, (send_hbm, keep_hbm) in enumerate(
            ((down_send_hbm, down_keep_hbm), (up_send_hbm, up_keep_hbm))
        ):
            for get in gets[k]:
                get.wait()
            for at in range(0, hidden, 256):
                span = slice(at, at + 256)
                value = times(turned_ref[k], other_ref[k, :, span])
                send_ref[k, :, span] = value[half:].astype(BF16)
                keep_ref[k, :, span] = value[:half].astype(BF16)
                if (at + 256) % chunk == 0:
                    done = slice(at + 256 - chunk, at + 256)
                    puts.append(copies.start(send_ref.at[k, :, done], send_hbm.at[:, done]))
                    puts.append(copies.start(keep_ref.at[k, :, done], keep_hbm.at[:, done]))
        for put in puts:
            put.wait()

    return kernel_call(
        body,
        "weight_products",
        (shape((half, hidden), BF16),) * 4,
        [VMEM, VMEM, VMEM, ANY, ANY, ANY, ANY, ANY, ANY],
        (ANY,) * 4,
        [
            pltpu.VMEM((2, width, 2 * seq), BF16),
            pltpu.VMEM((2, 2 * seq, hidden), BF16),
            pltpu.VMEM((2, half, hidden), BF16),
            pltpu.VMEM((2, half, hidden), BF16),
            pltpu.SemaphoreType.DMA((24,)),
        ],
    )(
        rows,
        grads,
        source_row,
        rows_turned,
        grads_turned,
        own_act,
        peer_act,
        own_pre,
        peer_pre,
    )


def forward_sum(act, w_down, after):
    seq, hidden = act.shape
    width = w_down.shape[1]

    def body(act_ref, w_down_hbm, out_ref, w_down_ref, sems):
        copies = Copies(sems)
        spans = [slice(at, at + 384) for at in range(0, width, 384)]
        gets = [copies.start(w_down_hbm.at[:, span], w_down_ref.at[:, span]) for span in spans]
        for span, get in zip(spans, gets):
            get.wait()
            out_ref[:, span] = times(act_ref[...], w_down_ref[:, span]).astype(BF16)

    return kernel_call(
        body,
        "forward_sum",
        shape((seq, width), BF16),
        [VMEM, ANY],
        VMEM,
        [pltpu.VMEM((hidden, width), BF16), pltpu.SemaphoreType.DMA((width // 384,))],
        after,
    )(act, w_down)


def gate(arrays, after):
    count = len(arrays)

    def body(*refs):
        del refs

    return pl.pallas_call(
        body,
        name="gate",
        out_shape=tuple(shape(array.shape, array.dtype) for array in arrays),
        in_specs=[ANY] * (count + len(after)),
        out_specs=(ANY,) * count,
        input_output_aliases={k: k for k in range(count)},
    )(*arrays, *after)


def branch_back(
    own_back, received, cotangent, middle, mod, w_out, own_sum, peer_sum, mp_at, after
):
    seq, width = cotangent.shape
    hidden = own_sum.shape[1]
    small_rows = -(-((2 * hidden + 2 * width) // LINE) // 16) * 16

    def body(
        own_back_hbm,
        received_hbm,
        cotangent_ref,
        middle_hbm,
        mod_ref,
        w_out_hbm,
        own_sum_ref,
        peer_sum_ref,
        mp_ref,
        grad_middle_hbm,
        branch_hbm,
        attended_hbm,
        sums_ref,
        small_ref,
        own_back_ref,
        received_ref,
        middle_ref,
        w_out_ref,
        grad_middle_ref,
        branch_ref,
        attended_ref,
        sems,
    ):
        copies = Copies(sems)
        gets = [
            copies.start(own_back_hbm, own_back_ref),
            copies.start(received_hbm, received_ref),
            copies.start(middle_hbm, middle_ref),
        ]
        get_w = copies.start(w_out_hbm, w_out_ref)
        puts = []
        for get in gets:
            get.wait()
        gain = 1.0 + mod_ref[0:1, 3 * width :]
        shift_sum = jnp.zeros((8, width), F32)
        scale_sum = jnp.zeros((8, width), F32)
        branch_sum = jnp.zeros((8, width), F32)
        down_sum = jnp.zeros((8, width), F32)

        def folded(rows):
            return jnp.sum(rows.reshape(ROWS // 8, 8, width), axis=0)

        for at in range(0, seq, ROWS):
            span = slice(at, at + ROWS)
            gradient = own_back_ref[span, :] + received_ref[span, :].astype(F32)
            normed, inverse = normalized(middle_ref[span, :])
            shift_sum = shift_sum + folded(gradient)
            scale_sum = scale_sum + folded(gradient * normed)
            above = cotangent_ref[span, :].astype(F32)
            down_sum = down_sum + folded(above)
            grad_middle = above + back_normalized(gradient * gain, normed, inverse)
            grad_middle_ref[span, :] = grad_middle
            branch = grad_middle.astype(BF16)
            branch_ref[span, :] = branch
            branch_sum = branch_sum + folded(branch.astype(F32))
        puts.append(copies.start(branch_ref, branch_hbm))
        puts.append(copies.start(grad_middle_ref, grad_middle_hbm))
        get_w.wait()
        for at in range(0, width, 384):
            attended_ref[:, at : at + 384] = times_transpose(
                branch_ref[...], w_out_ref[at : at + 384, :]
            ).astype(BF16)
        puts.append(copies.start(attended_ref, attended_hbm))
        mine = mp_ref[0]
        hidden_sum = own_sum_ref[...] + peer_sum_ref[...]
        pieces = [jnp.where(mine == slot, hidden_sum, 0.0) for slot in range(2)]
        pieces.append(jnp.sum(branch_sum, axis=0, keepdims=True))
        pieces.append(jnp.sum(down_sum, axis=0, keepdims=True))
        line = jnp.concatenate(pieces, axis=1)
        small_ref[...] = jnp.zeros(small_ref.shape, F32)
        for k in range(line.shape[1] // LINE):
            small_ref[k : k + 1, :] = line[:, k * LINE : (k + 1) * LINE]
        sums_ref[0:1, :] = jnp.sum(shift_sum, axis=0, keepdims=True)
        sums_ref[1:2, :] = jnp.sum(scale_sum, axis=0, keepdims=True)
        for put in puts:
            put.wait()

    return kernel_call(
        body,
        "branch_back",
        (
            shape((seq, width), F32),
            shape((seq, width), BF16),
            shape((seq, width), BF16),
            shape((8, width), F32),
            shape((small_rows, LINE), F32),
        ),
        [ANY, ANY, VMEM, ANY, VMEM, ANY, VMEM, VMEM, SMEM],
        (ANY, ANY, ANY, VMEM, VMEM),
        [
            pltpu.VMEM((seq, width), F32),
            pltpu.VMEM((seq, width), BF16),
            pltpu.VMEM((seq, width), F32),
            pltpu.VMEM((width, width), BF16),
            pltpu.VMEM((seq, width), F32),
            pltpu.VMEM((seq, width), BF16),
            pltpu.VMEM((seq, width), BF16),
            pltpu.SemaphoreType.DMA((8,)),
        ],
        after,
    )(own_back, received, cotangent, middle, mod, w_out, own_sum, peer_sum, mp_at)


def attention_back(attended, qkv, probs, small, cut, after):
    seq, width = attended.shape
    heads = probs.shape[0]
    size = width // heads
    grid = math.isqrt(seq)
    scale = size ** (-0.5)

    def body(
        above_ref,
        qkv_ref,
        probs_hbm,
        small_ref,
        projected_hbm,
        one_hbm,
        two_hbm,
        sums_ref,
        packed_ref,
        probs_ref,
        total_ref,
        projected_ref,
        sems,
    ):
        copies = Copies(sems)
        get_probs = [
            copies.start(probs_hbm.at[: heads // 4], probs_ref.at[: heads // 4]),
            copies.start(probs_hbm.at[heads // 4 :], probs_ref.at[heads // 4 :]),
        ]
        puts = []
        for head in range(heads):
            if head == 0:
                get_probs[0].wait()
            if head == heads // 4:
                get_probs[1].wait()
            start, stop, inside = head_window(head, size)
            query = qkv_ref[:, start:stop]
            key = qkv_ref[:, width + start : width + stop]
            value = qkv_ref[:, 2 * width + start : 2 * width + stop]
            above = jnp.where(inside, above_ref[:, start:stop], jnp.zeros((), BF16))
            low = probs_ref[head]
            weights = low.astype(F32)
            grad_probs = times_transpose(above, value)
            mean = jnp.sum(weights * grad_probs, axis=-1, keepdims=True)
            scores = (weights * (grad_probs - mean)).astype(BF16)
            grad_query = times(scores, key) * scale
            grad_key = contract_rows(scores, query) * scale
            grad_value = contract_rows(low, above)
            for k, value in enumerate((grad_query, grad_key, grad_value)):
                span = slice(k * width + start, k * width + stop)
                total_ref[:, span] = jnp.where(inside, value, total_ref[:, span])
            rows = head_bias_back(scores.astype(F32), grid)
            for k in range(4):
                packed_ref[k * heads + head : k * heads + head + 1, :] = rows[k]
        packed_ref[4 * heads :, :] = small_ref[...]
        projected_ref[...] = total_ref[...].astype(BF16)
        puts.append(copies.start(projected_ref.at[:, :cut], one_hbm))
        puts.append(copies.start(projected_ref.at[:, cut:], two_hbm))
        puts.append(copies.start(projected_ref, projected_hbm))
        for k, low in ((0, 0), (1, 2 * width)):
            total = jnp.zeros((8, width), F32)
            for at in range(0, seq, ROWS):
                rows = projected_ref[at : at + ROWS, low : low + width].astype(F32)
                total = total + jnp.sum(rows.reshape(ROWS // 8, 8, width), axis=0)
            sums_ref[k : k + 1, :] = jnp.sum(total, axis=0, keepdims=True)
        for put in puts:
            put.wait()

    return kernel_call(
        body,
        "attention_back",
        (
            shape((seq, 3 * width), BF16),
            shape((seq, cut), BF16),
            shape((seq, 3 * width - cut), BF16),
            shape((8, width), F32),
            shape((4 * heads + small.shape[0], seq), F32),
        ),
        [VMEM, VMEM, ANY, VMEM],
        (ANY, ANY, ANY, VMEM, VMEM),
        [
            pltpu.VMEM((heads, seq, seq), BF16),
            pltpu.VMEM((seq, 3 * width), F32),
            pltpu.VMEM((seq, 3 * width), BF16),
            pltpu.SemaphoreType.DMA((8,)),
        ],
        after,
    )(attended, qkv, probs, small)


def projection_products(turned_keep, turned_received, attended_pair, attn_pair, name, after):
    rows, seq = turned_keep.shape
    rows = rows // 2
    half = rows // 2
    pairs = [pair for pair in (attended_pair, attn_pair) if pair is not None]
    widths = [pair[0].shape[1] for pair in pairs]
    columns = sum(widths)

    def body(keep_hbm, received_hbm, *refs):
        count = 2 * len(pairs)
        factor_hbms = refs[:count]
        send_hbm, out_hbm, turned_ref, factor_ref, send_ref, out_ref, sems = refs[count:]
        copies = Copies(sems)
        gets = [
            copies.start(keep_hbm, turned_ref.at[:, :seq]),
            copies.start(received_hbm, turned_ref.at[:, seq:]),
        ]
        base = 0
        for k in range(len(pairs)):
            span = slice(base, base + widths[k])
            for part in range(2):
                gets.append(
                    copies.start(
                        factor_hbms[2 * k + part],
                        factor_ref.at[part * seq : (part + 1) * seq, span],
                    )
                )
            base += widths[k]
        for get in gets[:2]:
            get.wait()
        puts = []
        base = 0
        for k in range(len(pairs)):
            gets[2 + 2 * k].wait()
            gets[3 + 2 * k].wait()
            low = rows if pairs[k] is attended_pair else 0
            for at in range(base, base + widths[k], 256):
                span = slice(at, min(at + 256, base + widths[k]))
                value = times(turned_ref[low : low + rows, :], factor_ref[:, span])
                send_ref[:, span] = value[half:].astype(BF16)
                out_ref[:, span] = value[:half].astype(BF16)
            span = slice(base, base + widths[k])
            puts.append(copies.start(send_ref.at[:, span], send_hbm.at[:, span]))
            puts.append(copies.start(out_ref.at[:, span], out_hbm.at[:, span]))
            base += widths[k]
        for put in puts:
            put.wait()

    return kernel_call(
        body,
        name,
        (shape((half, columns), BF16),) * 2,
        [ANY] * (2 + 2 * len(pairs)),
        (ANY,) * 2,
        [
            pltpu.VMEM((2 * rows, 2 * seq), BF16),
            pltpu.VMEM((2 * seq, columns), BF16),
            pltpu.VMEM((half, columns), BF16),
            pltpu.VMEM((half, columns), BF16),
            pltpu.SemaphoreType.DMA((12,)),
        ],
        after,
    )(turned_keep, turned_received, *[factor for pair in pairs for factor in pair])


def latents_back(projected, w_qkv, latents, mod, grad_middle, sums, late_sums, steps, after):
    seq, width = latents.shape
    image_rows = -(-(6 * width // LINE + 1) // 16) * 16

    def body(
        projected_ref,
        w_qkv_hbm,
        latents_ref,
        mod_ref,
        grad_middle_ref,
        sums_ref,
        late_ref,
        steps_ref,
        out_ref,
        image_ref,
        w_qkv_ref,
        total_ref,
        sems,
    ):
        copies = Copies(sems)
        parts = 3
        chunk = width // parts
        gets = [
            copies.start(
                w_qkv_hbm.at[k * chunk : (k + 1) * chunk, :],
                w_qkv_ref.at[k * chunk : (k + 1) * chunk, :],
            )
            for k in range(parts)
        ]
        for k in range(parts):
            span = slice(k * chunk, (k + 1) * chunk)
            gets[k].wait()
            total_ref[:, span] = times_transpose(projected_ref[...], w_qkv_ref[span, :])
        gain = 1.0 + mod_ref[0:1, width : 2 * width]
        shift_sum = jnp.zeros((8, width), F32)
        scale_sum = jnp.zeros((8, width), F32)

        def folded(rows):
            return jnp.sum(rows.reshape(ROWS // 8, 8, width), axis=0)

        for at in range(0, seq, ROWS):
            span = slice(at, at + ROWS)
            gradient = total_ref[span, :]
            normed, inverse = normalized(latents_ref[span, :].astype(F32))
            shift_sum = shift_sum + folded(gradient)
            scale_sum = scale_sum + folded(gradient * normed)
            out_ref[span, :] = (
                grad_middle_ref[span, :] + back_normalized(gradient * gain, normed, inverse)
            ).astype(BF16)
        step = steps_ref[0]
        lanes = lax.broadcasted_iota(jnp.int32, (1, LINE), 1)
        high = lax.div(step, 32)
        low = step - 32 * high
        steps_row = jnp.where(lanes == 0, high, jnp.where(lanes == 1, low, 0)).astype(F32)
        line = jnp.concatenate(
            [
                jnp.sum(shift_sum, axis=0, keepdims=True),
                jnp.sum(scale_sum, axis=0, keepdims=True),
                sums_ref[0:1, :],
                sums_ref[1:2, :],
                late_ref[0:1, :],
                late_ref[1:2, :],
                steps_row,
            ],
            axis=1,
        )
        total_ref[0:image_rows, 0:LINE] = jnp.zeros((image_rows, LINE), F32)
        for k in range(line.shape[1] // LINE):
            total_ref[k : k + 1, 0:LINE] = line[:, k * LINE : (k + 1) * LINE]
        image_ref[...] = total_ref[0:image_rows, 0:LINE].astype(BF16)

    return kernel_call(
        body,
        "latents_back",
        (shape((seq, width), BF16), shape((image_rows, LINE), BF16)),
        [VMEM, ANY, VMEM, VMEM, VMEM, VMEM, VMEM, SMEM],
        (VMEM, VMEM),
        [
            pltpu.VMEM((width, 3 * width), BF16),
            pltpu.VMEM((seq, width), F32),
            pltpu.SemaphoreType.DMA((4,)),
        ],
        after,
    )(projected, w_qkv, latents, mod, grad_middle, sums, late_sums, steps)


def first_message(packed, images, after):
    rows, width = packed.shape
    tall = rows + images.shape[0]

    def body(packed_ref, images_ref, out_ref):
        out_ref[:rows, :] = packed_ref[...].astype(BF16)
        out_ref[rows:, :] = images_ref[...]

    return kernel_call(
        body, "first_message", shape((tall, width), BF16), [VMEM] * 2, VMEM, [], after
    )(packed, images)


def relative_blocks(bits, count):
    depth = len(bits)
    table = np.zeros((count,), np.int32)
    for place in range(count):
        for k, bit in enumerate(bits):
            table[place] |= ((place >> (depth - 1 - k)) & 1) << bit
    return table


def source_columns(blocks, mine, width):
    count = blocks.shape[0]
    size = width // count
    base = np.repeat(blocks, size)
    offset = np.tile(np.arange(size, dtype=np.int32), count)
    return ((jnp.asarray(base) ^ mine) * size + jnp.asarray(offset))[None, :]


def make_device(mesh):
    dp_size = mesh.shape["dp"]
    mp_size = mesh.shape["mp"]
    all_size = dp_size * mp_size
    dp_bits = dp_size.bit_length() - 1

    def swap(values, bit):
        if bit == 0:
            return lax.ppermute(values, "mp", [(i, i ^ 1) for i in range(mp_size)])
        return lax.ppermute(
            values, "dp", [(i, i ^ (1 << (bit - 1))) for i in range(dp_size)]
        )

    near_bits = list(range(1, dp_bits - 1))
    far_bits = [dp_bits, dp_bits - 1]
    far_size = 4
    near_size = dp_size // far_size
    far_groups = [[i + near_size * k for k in range(far_size)] for i in range(near_size)]
    dp_order = near_bits + far_bits
    all_order = [0, near_bits[0]] + near_bits[1:] + far_bits

    def finish(keep, received, bits, after=((), ())):
        received = [received]

        def part(low, high):
            value = keep[low:high].astype(F32)
            for item in received:
                value = value + item[low:high].astype(F32)
            return value.astype(BF16)

        high = keep.shape[0]
        sends = []
        for bit in bits:
            low = high // 2
            sends.append(part(low, high))
            received.append(swap(sends[-1], bit))
            if after[0]:
                received[-1:] = gate(received[-1:], after[0])
            after = after[1:] + ((),)
            high = low
        return part(0, high).reshape(far_size, high // far_size, -1), sends

    def far_scatter(blocks):
        rows = blocks.shape[1]
        tall = -(-rows // 8) * 8
        blocks = jnp.pad(blocks, ((0, 0), (0, tall - rows), (0, 0)))
        blocks = blocks.reshape(far_size * tall, -1)
        total = lax.psum_scatter(
            blocks, "dp", scatter_dimension=0, tiled=True, axis_index_groups=far_groups
        )
        return total[:rows].astype(F32)

    def on_device(
        latents,
        timesteps,
        rel_index,
        time_table,
        rel_bias,
        w_mod,
        b_mod,
        w_qkv,
        w_time,
        w_out,
        b_out,
        w_up,
        b_up,
        w_down,
        b_down,
        cotangent,
    ):
        seq_len, model_width = latents.shape
        head_count, entries = rel_bias.shape
        grid = math.isqrt(seq_len)
        table_size = time_table.shape[0]
        hidden_count = b_up.shape[0]
        dp_at = lax.axis_index("dp")
        mp_at = lax.axis_index("mp")
        device = dp_at * mp_size + mp_at
        share = model_width // all_size

        peer_cotangent = swap(cotangent, 0)
        near_mask = near_size - 1
        dp_blocks = relative_blocks([b - 1 for b in dp_order], dp_size)
        dp_source = source_columns(dp_blocks, dp_at & near_mask, model_width)
        all_blocks = relative_blocks(all_order, all_size)
        all_source = source_columns(
            all_blocks, device & (near_size * mp_size - 1), model_width
        )

        embedding = lax.dynamic_slice(time_table, (timesteps[0], 0), (1, model_width))
        (turned_keep, turned_send, qkv, probs, middle, mlp_in, mod) = front(
            latents,
            rel_index,
            rel_bias,
            embedding,
            b_mod[None, :],
            w_mod,
            w_qkv,
            w_time,
            w_out,
            b_out[None, :],
            all_source,
        )
        peer_in = swap(mlp_in, 0)
        bias_up = b_up[None, :]
        (own_act, own_pre, own_back, own_sum, own_out, rows_turned, grads_turned) = feed_forward(
            mlp_in, cotangent, w_up, bias_up, w_down, dp_source, True, (peer_cotangent,)
        )
        (peer_act, peer_pre, peer_back, peer_sum) = feed_forward(
            peer_in, peer_cotangent, w_up, bias_up, w_down, dp_source, False, (own_back,)
        )
        (turned_send,) = gate((turned_send,), (own_back,))
        turned_received = swap(turned_send, 0)
        back_received = swap(peer_back, 0)
        (down_send, down_keep, up_send, up_keep) = weight_products(
            peer_in,
            peer_cotangent,
            dp_source,
            rows_turned,
            grads_turned,
            own_act,
            peer_act,
            own_pre,
            peer_pre,
        )
        down_send, up_send = gate((down_send, up_send), (back_received,))
        peer_out = forward_sum(peer_act, w_down, (up_send,))
        first = near_bits[0]
        rest_bits = near_bits[1:]
        down_total, down_sends = finish(down_keep, swap(down_send, first), rest_bits)
        down_rows = far_scatter(down_total)
        up_total, up_sends = finish(up_keep, swap(up_send, first), rest_bits)
        out_received = swap(peer_out, 0)

        (grad_middle, branch, grad_attended, sums, small) = branch_back(
            own_back,
            back_received,
            cotangent,
            middle,
            mod,
            w_out,
            own_sum,
            peer_sum,
            mp_at[None].astype(jnp.int32),
            (down_sends[0], up_sends[0], peer_out),
        )
        peer_branch = swap(branch, 0)
        cut = 13 * model_width // 9
        (projected, proj_one, proj_two, late_sums, packed) = attention_back(
            grad_attended, qkv, probs, small, cut, (turned_received,)
        )
        peer_one = swap(proj_one, 0)
        peer_two = swap(proj_two, 0)
        (grad_latents, images) = latents_back(
            projected, w_qkv, latents, mod, grad_middle, sums, late_sums, timesteps, (down_total,)
        )
        one_send, one_keep = projection_products(
            turned_keep,
            turned_received,
            (branch, peer_branch),
            (proj_one, peer_one),
            "first_products",
            (images, up_total),
        )
        one_total, one_sends = finish(one_keep, swap(one_send, first), rest_bits)
        two_send, two_keep = projection_products(
            turned_keep,
            turned_received,
            None,
            (proj_two, peer_two),
            "second_products",
            (one_sends[0],),
        )
        two_total, two_sends = finish(
            two_keep, swap(two_send, first), rest_bits, ((one_total,), ())
        )
        grad_w_up = far_scatter(up_total)
        grad_w_down = down_rows.T
        proj_one = far_scatter(one_total)
        proj_two = far_scatter(two_total)
        grad_w_out = proj_one[:, :model_width]
        grad_w_qkv = jnp.concatenate([proj_one[:, model_width:], proj_two], axis=1)

        out = (
            middle + (own_out + out_received.astype(F32)) + b_down.astype(F32)[None, :]
        ).astype(BF16)

        small_rows = packed.shape[0]
        message = first_message(packed, images, (two_sends[0],))
        hops = 0
        for bit in [0, near_bits[0]] + far_bits + near_bits[1:]:
            if message is None:
                message = jnp.concatenate([packed.astype(BF16), images], axis=0)
            if hops == 3:
                (message,) = gate((message,), (one_total,))
            hops += 1
            got = swap(message, bit)
            message = None
            packed = packed + got[:small_rows].astype(F32)
            images = jnp.concatenate([images, got[small_rows:]], axis=0)

        corners = packed[: 4 * head_count].reshape(4, head_count, seq_len)
        grad_rel_bias = jnp.zeros((head_count, entries), F32)
        last = grid - 1
        for k, place in enumerate((last * grid, grid * grid - 1, 0, last)):
            select = rel_index[place][:, None] == lax.broadcasted_iota(
                jnp.int32, (seq_len, entries), 1
            )
            grad_rel_bias = grad_rel_bias + lax.dot_general(
                corners[k],
                select.astype(F32),
                (((1,), (0,)), ((), ())),
                precision=lax.Precision.HIGHEST,
                preferred_element_type=F32,
            )
        line = packed[4 * head_count :].reshape(-1)
        grad_b_up = lax.dynamic_slice(line, (mp_at * hidden_count,), (hidden_count,))
        base = mp_size * hidden_count
        grad_b_out = lax.dynamic_slice(line, (base + device * share,), (share,))
        grad_b_down = lax.dynamic_slice(line, (base + model_width + device * share,), (share,))

        images = images.reshape(all_size, -1)
        all_mod = images[:, : 4 * model_width]
        all_time = images[:, 4 * model_width : 6 * model_width]
        parts = images[:, 6 * model_width :].astype(F32)
        all_steps = (parts[:, 0] * 32.0 + parts[:, 1]).astype(jnp.int32)
        step_select = (
            all_steps[:, None] == lax.broadcasted_iota(jnp.int32, (all_size, table_size), 1)
        )
        own_columns = (
            lax.broadcasted_iota(jnp.int32, (model_width, share), 0)
            == device * share + lax.broadcasted_iota(jnp.int32, (model_width, share), 1)
        )
        own_table = times(time_table, own_columns.astype(BF16)).astype(BF16)
        own_embed = times(step_select.astype(BF16), own_table).astype(BF16)
        own_float = own_embed.astype(F32)
        own_silu, silu_pull = jax.vjp(jax.nn.silu, own_float)
        grad_w_mod = contract_rows(own_silu.astype(BF16), all_mod)
        grad_w_time = contract_rows(own_embed, all_time)
        mod_share = 4 * model_width // all_size
        grad_b_mod = lax.dynamic_slice(
            jnp.sum(all_mod.astype(F32), axis=0), (device * mod_share,), (mod_share,)
        )
        own_w_mod = lax.dynamic_slice(w_mod, (device * share, 0), (share, 4 * model_width))
        own_w_time = lax.dynamic_slice(w_time, (device * share, 0), (share, 2 * model_width))
        grad_embed = silu_pull(times_transpose(all_mod, own_w_mod))[0] + times_transpose(
            all_time, own_w_time
        )
        grad_table = lax.dot_general(
            step_select.astype(F32),
            grad_embed,
            (((0,), (0,)), ((), ())),
            precision=lax.Precision.HIGHEST,
            preferred_element_type=F32,
        )
        return (
            out,
            grad_latents,
            grad_table,
            grad_rel_bias,
            grad_w_mod,
            grad_b_mod,
            grad_w_qkv,
            grad_w_time,
            grad_w_out,
            grad_b_out,
            grad_w_up,
            grad_b_up,
            grad_w_down,
            grad_b_down,
        )

    return on_device


def solution(mesh):
    both = ("dp", "mp")
    in_specs = (
        P(both, None),
        P(both),
        P(),
        P(),
        P(),
        P(),
        P(),
        P(),
        P(),
        P(),
        P(),
        P(None, "mp"),
        P("mp"),
        P("mp", None),
        P(),
        P(both, None),
    )
    out_specs = (
        P(both, None),
        P(both, None),
        P(None, both),
        P(),
        P(both, None),
        P(both),
        P(both, None),
        P(both, None),
        P(both, None),
        P(both),
        P("dp", "mp"),
        P("mp"),
        P("mp", "dp"),
        P(both),
    )
    return jax.shard_map(
        make_device(mesh), mesh=mesh, in_specs=in_specs, out_specs=out_specs, check_vma=False
    )
```

```python
import functools
import math

import jax
import jax.numpy as jnp
import numpy as np
from jax import lax
from jax.experimental import pallas as pl
from jax.experimental.pallas import tpu as pltpu
from jax.sharding import PartitionSpec as P

EPSILON = 1e-06
F32 = jnp.float32
BF16 = jnp.bfloat16
ANY = pl.BlockSpec(memory_space=pl.ANY)
VMEM = pl.BlockSpec(memory_space=pltpu.VMEM)
SMEM = pl.BlockSpec(memory_space=pltpu.SMEM)
ROWS = 32
LINE = 256


def times(first_op, second_op):
    return jnp.dot(first_op, second_op, preferred_element_type=F32)


def contract_rows(first_op, second_op):
    return lax.dot_general(
        first_op, second_op, (((0,), (0,)), ((), ())), preferred_element_type=F32
    )


def times_transpose(first_op, second_op):
    return lax.dot_general(
        first_op, second_op, (((1,), (1,)), ((), ())), preferred_element_type=F32
    )


def kernel_call(body, name, out_shape, in_specs, out_specs, scratch, after=()):
    count = len(in_specs)
    extra = len(after)

    def run(*refs):
        body(*refs[:count], *refs[count + extra :])

    call = pl.pallas_call(
        run,
        name=name,
        out_shape=out_shape,
        in_specs=list(in_specs) + [ANY] * extra,
        out_specs=out_specs,
        scratch_shapes=scratch,
        compiler_params=pltpu.CompilerParams(vmem_limit_bytes=56 * 2**20),
        cost_estimate=pl.CostEstimate(flops=1000, bytes_accessed=1000, transcendentals=0),
    )
    return lambda *operands: call(*operands, *after)


def shape(dims, dtype):
    return jax.ShapeDtypeStruct(dims, dtype)


class Copies:
    def __init__(self, sems):
        self.sems = sems
        self.count = 0

    def start(self, source, target):
        copy = pltpu.make_async_copy(source, target, self.sems.at[self.count])
        self.count += 1
        copy.start()
        return copy


def normalized(rows):
    center = rows - jnp.mean(rows, axis=-1, keepdims=True)
    inverse = lax.rsqrt(jnp.mean(center * center, axis=-1, keepdims=True) + EPSILON)
    return center * inverse, inverse


def back_normalized(gradient, normed, inverse):
    return inverse * (
        gradient
        - jnp.mean(gradient, axis=-1, keepdims=True)
        - normed * jnp.mean(gradient * normed, axis=-1, keepdims=True)
    )


def turn_into(target_ref, first_column, source_row_ref, rows_ref, step=384):
    count, width = rows_ref.shape
    for at in range(0, width, step):
        places = lax.broadcasted_iota(jnp.int32, (width, step), 0)
        select = (places == source_row_ref[:, at : at + step]).astype(BF16)
        picked = times(rows_ref[...], select)
        target_ref[at : at + step, first_column : first_column + count] = picked.T.astype(BF16)


def head_window(head, head_size):
    low = head * head_size
    start = low // 128 * 128
    stop = -(-(low + head_size) // 128) * 128
    lanes = lax.broadcasted_iota(jnp.int32, (1, stop - start), 1) + start
    inside = jnp.logical_and(lanes >= low, lanes < low + head_size)
    return start, stop, inside


def corner_rows(rel_index_ref, grid):
    last = grid - 1
    for place in (last * grid, grid * grid - 1, 0, last):
        yield rel_index_ref[place : place + 1, :]


def entry_select(rel_index_ref, entries, grid):
    places = lax.broadcasted_iota(jnp.int32, (entries, grid * grid), 0)
    return [(places == row).astype(BF16) for row in corner_rows(rel_index_ref, grid)]


def head_bias(corners, head, grid):
    seq = grid * grid
    shape_ = (grid, seq)
    lanes = lax.broadcasted_iota(jnp.int32, shape_, 1)
    rows = lax.broadcasted_iota(jnp.int32, shape_, 0)
    later = lanes % grid >= rows

    def moved(corner, shift):
        wide = jnp.broadcast_to(corner[head : head + 1, :], shape_)
        return pltpu.roll(wide, shift, 1, stride=1, stride_axis=0)

    first = jnp.where(later, moved(corners[0], 0), moved(corners[1], seq - grid + 1))
    second = jnp.where(later, moved(corners[2], 0), moved(corners[3], seq - grid + 1))
    edge = (grid - 1) * grid
    blank = jnp.zeros(shape_, F32)
    wide = jnp.where(
        lax.broadcasted_iota(jnp.int32, (grid, 2 * seq), 1) < edge,
        jnp.concatenate([first, blank], axis=1),
        pltpu.roll(jnp.concatenate([second, blank], axis=1), edge, 1),
    )
    parts = [
        wide[:, grid * (grid - 1 - i) : grid * (grid - 1 - i) + seq] for i in range(grid)
    ]
    return jnp.concatenate(parts, axis=0)


def head_bias_back(score_grads, grid):
    seq = grid * grid
    edge = (grid - 1) * grid
    wide = jnp.zeros((grid, 2 * seq), F32)
    blank = jnp.zeros((grid, seq), F32)
    for i in range(grid):
        start = grid * (grid - 1 - i)
        rows = jnp.concatenate([score_grads[i * grid : (i + 1) * grid, :], blank], axis=1)
        wide = wide + (pltpu.roll(rows, start, 1) if start else rows)
    shape_ = (grid, seq)
    lanes = lax.broadcasted_iota(jnp.int32, shape_, 1)
    places = lax.broadcasted_iota(jnp.int32, shape_, 0)
    later = lanes % grid >= places
    first = jnp.where(lanes < edge, wide[:, :seq], 0.0)
    second = pltpu.roll(wide, 2 * seq - edge, 1)[:, :seq]

    def moved(values, shift):
        bit = 1
        while bit < grid:
            values = jnp.where(places & bit > 0, pltpu.roll(values, seq - bit, 1), values)
            bit *= 2
        total = jnp.sum(values, axis=0, keepdims=True)
        return pltpu.roll(total, shift, 1) if shift else total

    return [
        moved(jnp.where(later, first, 0.0), 0),
        moved(jnp.where(later, 0.0, first), grid - 1),
        moved(jnp.where(later, second, 0.0), 0),
        moved(jnp.where(later, 0.0, second), grid - 1),
    ]


def front(
    latents, rel_index, rel_bias, embed, b_mod, w_mod, w_qkv, w_time, w_out, b_out, source_row
):
    seq, width = latents.shape
    heads, entries = rel_bias.shape
    size = width // heads
    grid = math.isqrt(seq)
    scale = size ** (-0.5)

    def body(
        latents_hbm,
        rel_index_ref,
        rel_bias_ref,
        embed_ref,
        b_mod_ref,
        w_mod_hbm,
        w_qkv_hbm,
        w_time_hbm,
        w_out_hbm,
        b_out_ref,
        source_ref,
        turned_keep_hbm,
        turned_send_hbm,
        qkv_hbm,
        probs_hbm,
        middle_hbm,
        mlp_in_hbm,
        mod_ref,
        latents_ref,
        w_mod_ref,
        w_qkv_ref,
        w_time_ref,
        w_out_ref,
        attn_in_ref,
        attn_turned_ref,
        attended_turned_ref,
        qkv_ref,
        probs_ref,
        total_ref,
        attended_ref,
        middle_ref,
        mlp_in_ref,
        sems,
    ):
        copies = Copies(sems)
        half = 2 * width
        get_latents = copies.start(latents_hbm, latents_ref)
        get_mod_one = copies.start(w_mod_hbm.at[:, :half], w_mod_ref.at[:, :half])
        get_time = copies.start(w_time_hbm, w_time_ref)
        get_qkv = [
            copies.start(
                w_qkv_hbm.at[:, k * width : (k + 1) * width],
                w_qkv_ref.at[:, k * width : (k + 1) * width],
            )
            for k in range(3)
        ]
        get_out = copies.start(w_out_hbm, w_out_ref)
        get_mod_two = copies.start(w_mod_hbm.at[:, half:], w_mod_ref.at[:, half:])
        puts = []

        corners = [
            times(rel_bias_ref[...], select)
            for select in entry_select(rel_index_ref, entries, grid)
        ]
        embed_rows = jnp.broadcast_to(embed_ref[...].astype(F32), (16, width))
        silu = (embed_rows / (1.0 + jnp.exp(-embed_rows))).astype(BF16)

        get_mod_one.wait()
        mod_ref[:, :half] = times(silu, w_mod_ref[:, :half])[0:8] + b_mod_ref[
            :, :half
        ].astype(F32)
        get_latents.wait()
        shift = mod_ref[0:1, 0:width]
        gain = 1.0 + mod_ref[0:1, width:half]
        for at in range(0, seq, ROWS):
            normed, _ = normalized(latents_ref[at : at + ROWS, :].astype(F32))
            attn_in_ref[at : at + ROWS, :] = (normed * gain + shift).astype(BF16)
        get_time.wait()
        time_terms = times(embed_rows.astype(BF16), w_time_ref[...])[0:1]
        extra = (time_terms[:, :width], None, time_terms[:, width:])
        for k in range(3):
            get_qkv[k].wait()
            for at in range(0, width, 384):
                low = k * width + at
                value = times(attn_in_ref[...], w_qkv_ref[:, low : low + 384])
                if extra[k] is not None:
                    value = value + extra[k][:, at : at + 384]
                qkv_ref[:, low : low + 384] = value.astype(BF16)
        puts.append(copies.start(qkv_ref, qkv_hbm))

        for head in range(heads):
            start, stop, inside = head_window(head, size)
            query = jnp.where(inside, qkv_ref[:, start:stop], jnp.zeros((), BF16))
            key = qkv_ref[:, width + start : width + stop]
            value = qkv_ref[:, 2 * width + start : 2 * width + stop]
            scores = times_transpose(query, key) * scale + head_bias(corners, head, grid)
            exponent = jnp.exp(scores - jnp.max(scores, axis=-1, keepdims=True))
            probs = exponent / jnp.sum(exponent, axis=-1, keepdims=True)
            probs = probs.astype(BF16)
            probs_ref[head] = probs
            mixture = times(probs, value)
            total_ref[:, start:stop] = jnp.where(inside, mixture, total_ref[:, start:stop])
        puts.append(copies.start(probs_ref, probs_hbm))
        attended_ref[...] = total_ref[...].astype(BF16)

        get_mod_two.wait()
        mod_ref[:, half:] = times(silu, w_mod_ref[:, half:])[0:8] + b_mod_ref[
            :, half:
        ].astype(F32)
        get_out.wait()
        total_ref[...] = times(attended_ref[...], w_out_ref[...])
        shift = mod_ref[0:1, half : half + width]
        gain = 1.0 + mod_ref[0:1, half + width :]
        bias = b_out_ref[...].astype(F32)
        for at in range(0, seq, ROWS):
            span = slice(at, at + ROWS)
            middle = latents_ref[span, :].astype(F32) + (total_ref[span, :] + bias)
            middle_ref[span, :] = middle
            normed, _ = normalized(middle)
            mlp_in_ref[span, :] = (normed * gain + shift).astype(BF16)
        puts.append(copies.start(mlp_in_ref, mlp_in_hbm))
        puts.append(copies.start(middle_ref, middle_hbm))
        rows = width // 2
        for k, (turned_ref, values_ref) in enumerate(
            ((attn_turned_ref, attn_in_ref), (attended_turned_ref, attended_ref))
        ):
            turn_into(turned_ref, 0, source_ref, values_ref)
            span = slice(k * rows, (k + 1) * rows)
            puts.append(copies.start(turned_ref.at[:rows], turned_keep_hbm.at[span]))
            puts.append(copies.start(turned_ref.at[rows:], turned_send_hbm.at[span]))
        for put in puts:
            put.wait()

    return kernel_call(
        body,
        "front",
        (
            shape((width, seq), BF16),
            shape((width, seq), BF16),
            shape((seq, 3 * width), BF16),
            shape((heads, seq, seq), BF16),
            shape((seq, width), F32),
            shape((seq, width), BF16),
            shape((8, 4 * width), F32),
        ),
        [ANY, VMEM, VMEM, VMEM, VMEM, ANY, ANY, ANY, ANY, VMEM, VMEM],
        (ANY, ANY, ANY, ANY, ANY, ANY, VMEM),
        [
            pltpu.VMEM((seq, width), BF16),
            pltpu.VMEM((width, 4 * width), BF16),
            pltpu.VMEM((width, 3 * width), BF16),
            pltpu.VMEM((width, 2 * width), BF16),
            pltpu.VMEM((width, width), BF16),
            pltpu.VMEM((seq, width), BF16),
            pltpu.VMEM((width, seq), BF16),
            pltpu.VMEM((width, seq), BF16),
            pltpu.VMEM((seq, 3 * width), BF16),
            pltpu.VMEM((heads, seq, seq), BF16),
            pltpu.VMEM((seq, width), F32),
            pltpu.VMEM((seq, width), BF16),
            pltpu.VMEM((seq, width), F32),
            pltpu.VMEM((seq, width), BF16),
            pltpu.SemaphoreType.DMA((16,)),
        ],
    )(
        latents,
        rel_index,
        rel_bias,
        embed,
        b_mod,
        w_mod,
        w_qkv,
        w_time,
        w_out,
        b_out,
        source_row,
    )


def feed_forward(rows, grads, w_up, b_up, w_down, source_row, own, after=()):
    seq, width = rows.shape
    hidden = w_up.shape[1]
    step = 256
    parts = 3
    chunk = hidden // parts

    def body(*refs):
        (rows_ref, grads_ref, w_up_hbm, b_up_ref, w_down_hbm, source_ref) = refs[:6]
        if own:
            (act_hbm, pre_hbm, back_hbm, sum_ref, out_hbm, rows_turned_hbm, grads_turned_hbm) = refs[6:13]
            scratch = refs[13:]
        else:
            (act_hbm, pre_hbm, back_hbm, sum_ref) = refs[6:10]
            scratch = refs[10:]
        (w_up_ref, w_down_ref, act_ref, pre_ref, back_ref, sems) = scratch[:6]
        copies = Copies(sems)
        gets = []
        for k in range(parts):
            span = slice(k * chunk, (k + 1) * chunk)
            gets.append(copies.start(w_up_hbm.at[:, span], w_up_ref.at[:, span]))
            gets.append(copies.start(w_down_hbm.at[span, :], w_down_ref.at[span, :]))
        puts = []
        if own:
            out_ref, rows_turned_ref, grads_turned_ref = scratch[6:9]
            turn_into(rows_turned_ref, 0, source_ref, rows_ref)
            puts.append(copies.start(rows_turned_ref, rows_turned_hbm))
            turn_into(grads_turned_ref, 0, source_ref, grads_ref)
            puts.append(copies.start(grads_turned_ref, grads_turned_hbm))
        for at in range(0, hidden, step):
            if at % chunk == 0:
                gets[2 * (at // chunk)].wait()
                gets[2 * (at // chunk) + 1].wait()
            span = slice(at, at + step)
            pre_act = times(rows_ref[...], w_up_ref[:, span]) + b_up_ref[:, span].astype(F32)
            grad_act = times_transpose(grads_ref[...], w_down_ref[span, :])
            below = 0.5 * (1.0 + lax.erf(pre_act * math.sqrt(0.5)))
            slope = below + pre_act * (
                jnp.exp(-0.5 * pre_act * pre_act) * (1.0 / math.sqrt(2.0 * math.pi))
            )
            act_ref[:, span] = (pre_act * below).astype(BF16)
            grad_pre = (slope * grad_act).astype(BF16)
            pre_ref[:, span] = grad_pre
            sum_ref[:, span] = jnp.sum(grad_pre.astype(F32), axis=0, keepdims=True)
        puts.append(copies.start(act_ref, act_hbm))
        puts.append(copies.start(pre_ref, pre_hbm))
        for at in range(0, width, 384):
            span = slice(at, at + 384)
            back_ref[:, span] = times_transpose(pre_ref[...], w_up_ref[span, :]).astype(
                back_ref.dtype
            )
        puts.append(copies.start(back_ref, back_hbm))
        if own:
            for at in range(0, width, 384):
                span = slice(at, at + 384)
                out_ref[:, span] = times(act_ref[...], w_down_ref[:, span])
            puts.append(copies.start(out_ref, out_hbm))
        for put in puts:
            put.wait()

    kind = F32 if own else BF16
    outs = [
        shape((seq, hidden), BF16),
        shape((seq, hidden), BF16),
        shape((seq, width), kind),
        shape((1, hidden), F32),
    ]
    specs = [ANY, ANY, ANY, VMEM]
    scratch = [
        pltpu.VMEM((width, hidden), BF16),
        pltpu.VMEM((hidden, width), BF16),
        pltpu.VMEM((seq, hidden), BF16),
        pltpu.VMEM((seq, hidden), BF16),
        pltpu.VMEM((seq, width), kind),
        pltpu.SemaphoreType.DMA((16,)),
    ]
    if own:
        outs += [shape((seq, width), F32), shape((width, seq), BF16), shape((width, seq), BF16)]
        specs += [ANY, ANY, ANY]
        scratch += [
            pltpu.VMEM((seq, width), F32),
            pltpu.VMEM((width, seq), BF16),
            pltpu.VMEM((width, seq), BF16),
        ]
    return kernel_call(
        body,
        "own_hidden" if own else "peer_hidden",
        tuple(outs),
        [VMEM, VMEM, ANY, VMEM, ANY, VMEM],
        tuple(specs),
        scratch,
        after,
    )(rows, grads, w_up, b_up, w_down, source_row)


def weight_products(
    rows, grads, source_row, rows_turned, grads_turned, own_act, peer_act, own_pre, peer_pre
):
    seq, width = rows.shape
    hidden = own_act.shape[1]
    half = width // 2
    parts = 3
    chunk = hidden // parts

    def body(
        rows_ref,
        grads_ref,
        source_ref,
        rows_turned_hbm,
        grads_turned_hbm,
        own_act_hbm,
        peer_act_hbm,
        own_pre_hbm,
        peer_pre_hbm,
        down_high_hbm,
        down_low_hbm,
        down_keep_hbm,
        up_high_hbm,
        up_low_hbm,
        up_keep_hbm,
        turned_ref,
        other_ref,
        send_ref,
        keep_ref,
        sems,
    ):
        copies = Copies(sems)
        gets = []
        for k, (turned, own, peer) in enumerate(
            (
                (grads_turned_hbm, own_act_hbm, peer_act_hbm),
                (rows_turned_hbm, own_pre_hbm, peer_pre_hbm),
            )
        ):
            gets.append(
                [
                    copies.start(turned, turned_ref.at[k, :, :seq]),
                    copies.start(own, other_ref.at[k, :seq, :]),
                    copies.start(peer, other_ref.at[k, seq:, :]),
                ]
            )
        puts = []
        turn_into(turned_ref.at[0], seq, source_ref, grads_ref)
        turn_into(turned_ref.at[1], seq, source_ref, rows_ref)
        quarter = half // 2
        for k, (high_hbm, low_hbm, keep_hbm) in enumerate(
            (
                (down_high_hbm, down_low_hbm, down_keep_hbm),
                (up_high_hbm, up_low_hbm, up_keep_hbm),
            )
        ):
            for get in gets[k]:
                get.wait()
            for at in range(0, hidden, 256):
                span = slice(at, at + 256)
                value = times(turned_ref[k], other_ref[k, :, span])
                send_ref[k, :, span] = value[half:].astype(BF16)
                keep_ref[k, :, span] = value[:half].astype(BF16)
                if (at + 256) % chunk == 0:
                    done = slice(at + 256 - chunk, at + 256)
                    puts.append(
                        copies.start(send_ref.at[k, quarter:, done], high_hbm.at[:, done])
                    )
                    puts.append(
                        copies.start(send_ref.at[k, :quarter, done], low_hbm.at[:, done])
                    )
                    puts.append(copies.start(keep_ref.at[k, :, done], keep_hbm.at[:, done]))
        for put in puts:
            put.wait()

    return kernel_call(
        body,
        "weight_products",
        (
            shape((half // 2, hidden), BF16),
            shape((half // 2, hidden), BF16),
            shape((half, hidden), BF16),
        )
        * 2,
        [VMEM, VMEM, VMEM, ANY, ANY, ANY, ANY, ANY, ANY],
        (ANY,) * 6,
        [
            pltpu.VMEM((2, width, 2 * seq), BF16),
            pltpu.VMEM((2, 2 * seq, hidden), BF16),
            pltpu.VMEM((2, half, hidden), BF16),
            pltpu.VMEM((2, half, hidden), BF16),
            pltpu.SemaphoreType.DMA((32,)),
        ],
    )(
        rows,
        grads,
        source_row,
        rows_turned,
        grads_turned,
        own_act,
        peer_act,
        own_pre,
        peer_pre,
    )


def forward_sum(act, w_down, after):
    seq, hidden = act.shape
    width = w_down.shape[1]

    def body(act_ref, w_down_hbm, out_ref, w_down_ref, sems):
        copies = Copies(sems)
        spans = [slice(at, at + 384) for at in range(0, width, 384)]
        gets = [copies.start(w_down_hbm.at[:, span], w_down_ref.at[:, span]) for span in spans]
        for span, get in zip(spans, gets):
            get.wait()
            out_ref[:, span] = times(act_ref[...], w_down_ref[:, span]).astype(BF16)

    return kernel_call(
        body,
        "forward_sum",
        shape((seq, width), BF16),
        [VMEM, ANY],
        VMEM,
        [pltpu.VMEM((hidden, width), BF16), pltpu.SemaphoreType.DMA((width // 384,))],
        after,
    )(act, w_down)


def gate(arrays, after):
    count = len(arrays)

    def body(*refs):
        del refs

    return pl.pallas_call(
        body,
        name="gate",
        out_shape=tuple(shape(array.shape, array.dtype) for array in arrays),
        in_specs=[ANY] * (count + len(after)),
        out_specs=(ANY,) * count,
        input_output_aliases={k: k for k in range(count)},
    )(*arrays, *after)


def branch_back(
    own_back, received, cotangent, middle, mod, w_out, own_sum, peer_sum, mp_at, after
):
    seq, width = cotangent.shape
    hidden = own_sum.shape[1]
    small_rows = -(-((2 * hidden + 2 * width) // LINE) // 16) * 16

    def body(
        own_back_hbm,
        received_hbm,
        cotangent_ref,
        middle_hbm,
        mod_ref,
        w_out_hbm,
        own_sum_ref,
        peer_sum_ref,
        mp_ref,
        grad_middle_hbm,
        branch_hbm,
        attended_hbm,
        sums_ref,
        small_ref,
        own_back_ref,
        received_ref,
        middle_ref,
        w_out_ref,
        grad_middle_ref,
        branch_ref,
        attended_ref,
        sems,
    ):
        copies = Copies(sems)
        gets = [
            copies.start(own_back_hbm, own_back_ref),
            copies.start(received_hbm, received_ref),
            copies.start(middle_hbm, middle_ref),
        ]
        get_w = copies.start(w_out_hbm, w_out_ref)
        puts = []
        for get in gets:
            get.wait()
        gain = 1.0 + mod_ref[0:1, 3 * width :]
        shift_sum = jnp.zeros((8, width), F32)
        scale_sum = jnp.zeros((8, width), F32)
        branch_sum = jnp.zeros((8, width), F32)
        down_sum = jnp.zeros((8, width), F32)

        def folded(rows):
            return jnp.sum(rows.reshape(ROWS // 8, 8, width), axis=0)

        for at in range(0, seq, ROWS):
            span = slice(at, at + ROWS)
            gradient = own_back_ref[span, :] + received_ref[span, :].astype(F32)
            normed, inverse = normalized(middle_ref[span, :])
            shift_sum = shift_sum + folded(gradient)
            scale_sum = scale_sum + folded(gradient * normed)
            above = cotangent_ref[span, :].astype(F32)
            down_sum = down_sum + folded(above)
            grad_middle = above + back_normalized(gradient * gain, normed, inverse)
            grad_middle_ref[span, :] = grad_middle
            branch = grad_middle.astype(BF16)
            branch_ref[span, :] = branch
            branch_sum = branch_sum + folded(branch.astype(F32))
        puts.append(copies.start(branch_ref, branch_hbm))
        puts.append(copies.start(grad_middle_ref, grad_middle_hbm))
        get_w.wait()
        for at in range(0, width, 384):
            attended_ref[:, at : at + 384] = times_transpose(
                branch_ref[...], w_out_ref[at : at + 384, :]
            ).astype(BF16)
        puts.append(copies.start(attended_ref, attended_hbm))
        mine = mp_ref[0]
        hidden_sum = own_sum_ref[...] + peer_sum_ref[...]
        pieces = [jnp.where(mine == slot, hidden_sum, 0.0) for slot in range(2)]
        pieces.append(jnp.sum(branch_sum, axis=0, keepdims=True))
        pieces.append(jnp.sum(down_sum, axis=0, keepdims=True))
        line = jnp.concatenate(pieces, axis=1)
        small_ref[...] = jnp.zeros(small_ref.shape, F32)
        for k in range(line.shape[1] // LINE):
            small_ref[k : k + 1, :] = line[:, k * LINE : (k + 1) * LINE]
        sums_ref[0:1, :] = jnp.sum(shift_sum, axis=0, keepdims=True)
        sums_ref[1:2, :] = jnp.sum(scale_sum, axis=0, keepdims=True)
        for put in puts:
            put.wait()

    return kernel_call(
        body,
        "branch_back",
        (
            shape((seq, width), F32),
            shape((seq, width), BF16),
            shape((seq, width), BF16),
            shape((8, width), F32),
            shape((small_rows, LINE), F32),
        ),
        [ANY, ANY, VMEM, ANY, VMEM, ANY, VMEM, VMEM, SMEM],
        (ANY, ANY, ANY, VMEM, VMEM),
        [
            pltpu.VMEM((seq, width), F32),
            pltpu.VMEM((seq, width), BF16),
            pltpu.VMEM((seq, width), F32),
            pltpu.VMEM((width, width), BF16),
            pltpu.VMEM((seq, width), F32),
            pltpu.VMEM((seq, width), BF16),
            pltpu.VMEM((seq, width), BF16),
            pltpu.SemaphoreType.DMA((8,)),
        ],
        after,
    )(own_back, received, cotangent, middle, mod, w_out, own_sum, peer_sum, mp_at)


def attention_back(attended, qkv, probs, small, cut, after):
    seq, width = attended.shape
    heads = probs.shape[0]
    size = width // heads
    grid = math.isqrt(seq)
    scale = size ** (-0.5)

    def body(
        above_ref,
        qkv_ref,
        probs_hbm,
        small_ref,
        projected_hbm,
        one_hbm,
        two_hbm,
        sums_ref,
        packed_ref,
        probs_ref,
        total_ref,
        projected_ref,
        sems,
    ):
        copies = Copies(sems)
        get_probs = [
            copies.start(probs_hbm.at[: heads // 4], probs_ref.at[: heads // 4]),
            copies.start(probs_hbm.at[heads // 4 :], probs_ref.at[heads // 4 :]),
        ]
        puts = []
        for head in range(heads):
            if head == 0:
                get_probs[0].wait()
            if head == heads // 4:
                get_probs[1].wait()
            start, stop, inside = head_window(head, size)
            query = qkv_ref[:, start:stop]
            key = qkv_ref[:, width + start : width + stop]
            value = qkv_ref[:, 2 * width + start : 2 * width + stop]
            above = jnp.where(inside, above_ref[:, start:stop], jnp.zeros((), BF16))
            low = probs_ref[head]
            weights = low.astype(F32)
            grad_probs = times_transpose(above, value)
            mean = jnp.sum(weights * grad_probs, axis=-1, keepdims=True)
            scores = (weights * (grad_probs - mean)).astype(BF16)
            grad_query = times(scores, key) * scale
            grad_key = contract_rows(scores, query) * scale
            grad_value = contract_rows(low, above)
            for k, value in enumerate((grad_query, grad_key, grad_value)):
                span = slice(k * width + start, k * width + stop)
                total_ref[:, span] = jnp.where(inside, value, total_ref[:, span])
            rows = head_bias_back(scores.astype(F32), grid)
            for k in range(4):
                packed_ref[k * heads + head : k * heads + head + 1, :] = rows[k]
        packed_ref[4 * heads :, :] = small_ref[...]
        projected_ref[...] = total_ref[...].astype(BF16)
        puts.append(copies.start(projected_ref.at[:, :cut], one_hbm))
        puts.append(copies.start(projected_ref.at[:, cut:], two_hbm))
        puts.append(copies.start(projected_ref, projected_hbm))
        for k, low in ((0, 0), (1, 2 * width)):
            total = jnp.zeros((8, width), F32)
            for at in range(0, seq, ROWS):
                rows = projected_ref[at : at + ROWS, low : low + width].astype(F32)
                total = total + jnp.sum(rows.reshape(ROWS // 8, 8, width), axis=0)
            sums_ref[k : k + 1, :] = jnp.sum(total, axis=0, keepdims=True)
        for put in puts:
            put.wait()

    return kernel_call(
        body,
        "attention_back",
        (
            shape((seq, 3 * width), BF16),
            shape((seq, cut), BF16),
            shape((seq, 3 * width - cut), BF16),
            shape((8, width), F32),
            shape((4 * heads + small.shape[0], seq), F32),
        ),
        [VMEM, VMEM, ANY, VMEM],
        (ANY, ANY, ANY, VMEM, VMEM),
        [
            pltpu.VMEM((heads, seq, seq), BF16),
            pltpu.VMEM((seq, 3 * width), F32),
            pltpu.VMEM((seq, 3 * width), BF16),
            pltpu.SemaphoreType.DMA((8,)),
        ],
        after,
    )(attended, qkv, probs, small)


def projection_products(turned_keep, turned_received, attended_pair, attn_pair, name, after):
    rows, seq = turned_keep.shape
    rows = rows // 2
    half = rows // 2
    pairs = [pair for pair in (attended_pair, attn_pair) if pair is not None]
    widths = [pair[0].shape[1] for pair in pairs]
    columns = sum(widths)

    def body(keep_hbm, received_hbm, *refs):
        count = 2 * len(pairs)
        factor_hbms = refs[:count]
        high_hbm, low_hbm, out_hbm, turned_ref, factor_ref, send_ref, out_ref, sems = refs[count:]
        copies = Copies(sems)
        gets = [
            copies.start(keep_hbm, turned_ref.at[:, :seq]),
            copies.start(received_hbm, turned_ref.at[:, seq:]),
        ]
        base = 0
        for k in range(len(pairs)):
            span = slice(base, base + widths[k])
            for part in range(2):
                gets.append(
                    copies.start(
                        factor_hbms[2 * k + part],
                        factor_ref.at[part * seq : (part + 1) * seq, span],
                    )
                )
            base += widths[k]
        for get in gets[:2]:
            get.wait()
        puts = []
        base = 0
        for k in range(len(pairs)):
            gets[2 + 2 * k].wait()
            gets[3 + 2 * k].wait()
            low = rows if pairs[k] is attended_pair else 0
            for at in range(base, base + widths[k], 256):
                span = slice(at, min(at + 256, base + widths[k]))
                value = times(turned_ref[low : low + rows, :], factor_ref[:, span])
                send_ref[:, span] = value[half:].astype(BF16)
                out_ref[:, span] = value[:half].astype(BF16)
            span = slice(base, base + widths[k])
            puts.append(copies.start(send_ref.at[half // 2 :, span], high_hbm.at[:, span]))
            puts.append(copies.start(send_ref.at[: half // 2, span], low_hbm.at[:, span]))
            puts.append(copies.start(out_ref.at[:, span], out_hbm.at[:, span]))
            base += widths[k]
        for put in puts:
            put.wait()

    return kernel_call(
        body,
        name,
        (
            shape((half // 2, columns), BF16),
            shape((half // 2, columns), BF16),
            shape((half, columns), BF16),
        ),
        [ANY] * (2 + 2 * len(pairs)),
        (ANY,) * 3,
        [
            pltpu.VMEM((2 * rows, 2 * seq), BF16),
            pltpu.VMEM((2 * seq, columns), BF16),
            pltpu.VMEM((half, columns), BF16),
            pltpu.VMEM((half, columns), BF16),
            pltpu.SemaphoreType.DMA((12,)),
        ],
        after,
    )(turned_keep, turned_received, *[factor for pair in pairs for factor in pair])


def latents_back(projected, w_qkv, latents, mod, grad_middle, sums, late_sums, steps, after):
    seq, width = latents.shape
    image_rows = -(-(6 * width // LINE + 1) // 16) * 16

    def body(
        projected_ref,
        w_qkv_hbm,
        latents_ref,
        mod_ref,
        grad_middle_ref,
        sums_ref,
        late_ref,
        steps_ref,
        out_ref,
        image_ref,
        w_qkv_ref,
        total_ref,
        sems,
    ):
        copies = Copies(sems)
        parts = 3
        chunk = width // parts
        gets = [
            copies.start(
                w_qkv_hbm.at[k * chunk : (k + 1) * chunk, :],
                w_qkv_ref.at[k * chunk : (k + 1) * chunk, :],
            )
            for k in range(parts)
        ]
        for k in range(parts):
            span = slice(k * chunk, (k + 1) * chunk)
            gets[k].wait()
            total_ref[:, span] = times_transpose(projected_ref[...], w_qkv_ref[span, :])
        gain = 1.0 + mod_ref[0:1, width : 2 * width]
        shift_sum = jnp.zeros((8, width), F32)
        scale_sum = jnp.zeros((8, width), F32)

        def folded(rows):
            return jnp.sum(rows.reshape(ROWS // 8, 8, width), axis=0)

        for at in range(0, seq, ROWS):
            span = slice(at, at + ROWS)
            gradient = total_ref[span, :]
            normed, inverse = normalized(latents_ref[span, :].astype(F32))
            shift_sum = shift_sum + folded(gradient)
            scale_sum = scale_sum + folded(gradient * normed)
            out_ref[span, :] = (
                grad_middle_ref[span, :] + back_normalized(gradient * gain, normed, inverse)
            ).astype(BF16)
        step = steps_ref[0]
        lanes = lax.broadcasted_iota(jnp.int32, (1, LINE), 1)
        high = lax.div(step, 32)
        low = step - 32 * high
        steps_row = jnp.where(lanes == 0, high, jnp.where(lanes == 1, low, 0)).astype(F32)
        line = jnp.concatenate(
            [
                jnp.sum(shift_sum, axis=0, keepdims=True),
                jnp.sum(scale_sum, axis=0, keepdims=True),
                sums_ref[0:1, :],
                sums_ref[1:2, :],
                late_ref[0:1, :],
                late_ref[1:2, :],
                steps_row,
            ],
            axis=1,
        )
        total_ref[0:image_rows, 0:LINE] = jnp.zeros((image_rows, LINE), F32)
        for k in range(line.shape[1] // LINE):
            total_ref[k : k + 1, 0:LINE] = line[:, k * LINE : (k + 1) * LINE]
        image_ref[...] = total_ref[0:image_rows, 0:LINE].astype(BF16)

    return kernel_call(
        body,
        "latents_back",
        (shape((seq, width), BF16), shape((image_rows, LINE), BF16)),
        [VMEM, ANY, VMEM, VMEM, VMEM, VMEM, VMEM, SMEM],
        (VMEM, VMEM),
        [
            pltpu.VMEM((width, 3 * width), BF16),
            pltpu.VMEM((seq, width), F32),
            pltpu.SemaphoreType.DMA((4,)),
        ],
        after,
    )(projected, w_qkv, latents, mod, grad_middle, sums, late_sums, steps)


def first_message(packed, images, after):
    rows, width = packed.shape
    tall = rows + images.shape[0]

    def body(packed_ref, images_ref, out_ref):
        out_ref[:rows, :] = packed_ref[...].astype(BF16)
        out_ref[rows:, :] = images_ref[...]

    return kernel_call(
        body, "first_message", shape((tall, width), BF16), [VMEM] * 2, VMEM, [], after
    )(packed, images)


def next_message(packed, message, received, after):
    rows, width = packed.shape
    count = message.shape[0] - rows

    def body(packed_ref, message_ref, received_ref, sum_ref, out_ref):
        total = packed_ref[...] + received_ref[:rows, :].astype(F32)
        sum_ref[...] = total
        out_ref[:rows, :] = total.astype(BF16)
        out_ref[rows : rows + count, :] = message_ref[rows:, :]
        out_ref[rows + count :, :] = received_ref[rows:, :]

    return kernel_call(
        body,
        "next_message",
        (shape((rows, width), F32), shape((rows + 2 * count, width), BF16)),
        [VMEM] * 3,
        (VMEM, VMEM),
        [],
        after,
    )(packed, message, received)


def split_three(values):
    first = values.astype(BF16)
    rest = values - first.astype(F32)
    second = rest.astype(BF16)
    third = (rest - second.astype(F32)).astype(BF16)
    return first, second, third


def small_gradients(
    packed, message, received, rel_index, time_table, own_w_mod, own_w_time, place, heads, entries, images, mp_size, after
):
    rows, line = packed.shape
    table_size, width = time_table.shape
    share = own_w_mod.shape[0]
    seq = rel_index.shape[0]
    grid = math.isqrt(seq)
    count = message.shape[0] - rows
    each = 2 * count // images
    mod_share = 4 * width // images

    def body(
        place_ref,
        packed_ref,
        message_ref,
        received_ref,
        rel_index_ref,
        time_table_ref,
        w_mod_ref,
        w_time_ref,
        bias_ref,
        w_mod_out,
        b_mod_out,
        w_time_out,
        table_out,
        lines_out,
        images_ref,
    ):
        device = place_ref[0]
        total = packed_ref[...] + received_ref[:rows, :].astype(F32)
        for k in range(line // 128):
            lanes = slice(k * 128, (k + 1) * 128)
            images_ref[k, :count, :] = message_ref[rows:, lanes].astype(F32)
            images_ref[k, count:, :] = received_ref[rows:, lanes].astype(F32)

        def piece(k):
            parts = [
                images_ref.at[half][pl.ds(k, images, stride=each), :]
                for half in range(line // 128)
            ]
            return jnp.concatenate(parts, axis=1)

        parts = piece(6 * width // line)
        steps = (parts[:, 0:1] * 32.0 + parts[:, 1:2]).astype(jnp.int32)
        step_select = (
            lax.broadcasted_iota(jnp.int32, (images, table_size), 1) == steps
        ).astype(BF16)
        own_columns = lax.broadcasted_iota(
            jnp.int32, (width, 128), 0
        ) == device * share + lax.broadcasted_iota(jnp.int32, (width, 128), 1)
        own_table = times(time_table_ref[...], own_columns.astype(BF16)).astype(BF16)
        embed = times(step_select, own_table)
        gate_ = 1.0 / (1.0 + jnp.exp(-embed))
        silu = (embed * gate_).astype(BF16)
        embed_low = embed.astype(BF16)
        slope = gate_ * (1.0 + embed * (1.0 - gate_))

        grad_silu = jnp.zeros((images, share), F32)
        sums = []
        for k in range(4 * width // line):
            span = slice(k * line, (k + 1) * line)
            values = piece(k)
            low = values.astype(BF16)
            w_mod_out[:, span] = contract_rows(silu, low)[:share]
            grad_silu = grad_silu + times_transpose(low, w_mod_ref[:, span])
            sums.append(jnp.sum(values, axis=0, keepdims=True))
        grad_embed = jnp.zeros((images, share), F32)
        for k in range(2 * width // line):
            span = slice(k * line, (k + 1) * line)
            low = piece(4 * width // line + k).astype(BF16)
            w_time_out[:, span] = contract_rows(embed_low, low)[:share]
            grad_embed = grad_embed + times_transpose(low, w_time_ref[:, span])
        grad_embed = grad_embed + slope[:, :share] * grad_silu
        first, second, third = split_three(grad_embed)
        table_out[...] = (
            contract_rows(step_select, third)
            + contract_rows(step_select, second)
            + contract_rows(step_select, first)
        )
        total_mod = jnp.concatenate(sums, axis=1)
        b_mod_out[...] = pltpu.roll(total_mod, 4 * width - device * mod_share, 1)[:, :mod_share]

        bias = jnp.zeros((3 * heads, entries), F32)
        for k, select in enumerate(entry_select(rel_index_ref, entries, grid)):
            corner = total[k * heads : (k + 1) * heads, :]
            stacked = jnp.concatenate(list(split_three(corner)), axis=0)
            bias = bias + times_transpose(stacked, select)
        bias_ref[...] = bias[2 * heads :] + bias[heads : 2 * heads] + bias[:heads]
        lines_out[...] = total[4 * heads :, :]

    return kernel_call(
        body,
        "small_gradients",
        (
            shape((heads, entries), F32),
            shape((share, 4 * width), F32),
            shape((1, mod_share), F32),
            shape((share, 2 * width), F32),
            shape((table_size, share), F32),
            shape((rows - 4 * heads, line), F32),
        ),
        [SMEM] + [VMEM] * 7,
        (VMEM,) * 6,
        [pltpu.VMEM((line // 128, 2 * count, 128), F32)],
        after,
    )(place, packed, message, received, rel_index, time_table, own_w_mod, own_w_time)


def relative_blocks(bits, count):
    depth = len(bits)
    table = np.zeros((count,), np.int32)
    for place in range(count):
        for k, bit in enumerate(bits):
            table[place] |= ((place >> (depth - 1 - k)) & 1) << bit
    return table


def source_columns(blocks, mine, width):
    count = blocks.shape[0]
    size = width // count
    base = np.repeat(blocks, size)
    offset = np.tile(np.arange(size, dtype=np.int32), count)
    return ((jnp.asarray(base) ^ mine) * size + jnp.asarray(offset))[None, :]


def make_device(mesh):
    dp_size = mesh.shape["dp"]
    mp_size = mesh.shape["mp"]
    all_size = dp_size * mp_size
    dp_bits = dp_size.bit_length() - 1

    def swap(values, bit):
        if bit == 0:
            return lax.ppermute(values, "mp", [(i, i ^ 1) for i in range(mp_size)])
        return lax.ppermute(
            values, "dp", [(i, i ^ (1 << (bit - 1))) for i in range(dp_size)]
        )

    core = 1
    rest_bits = list(range(2, dp_bits + 1))
    dp_order = [core] + rest_bits
    all_order = [0, core] + rest_bits

    class Sequence:
        def __init__(self):
            self.last = ()

        def take(self, *arrays):
            return gate(arrays, self.last) if self.last else arrays

        def mark(self, *arrays):
            self.last = arrays

    class Halving:
        def __init__(self, order, high, low, keep):
            self.order = order
            self.keep = keep
            self.high_piece = swap(high, core)
            self.low_piece = swap(low, core)
            self.received = []
            self.rows = keep.shape[0]
            self.bits = list(rest_bits)
            self.pending = None
            self.result = None

        def part(self, low, high):
            value = self.keep[low:high].astype(F32)
            if self.high_piece is not None:
                size = self.high_piece.shape[0]
                value = value + self.high_piece[low - size : high - size].astype(F32)
            else:
                value = value + self.low_piece[low:high].astype(F32)
            for item in self.received:
                value = value + item[low:high].astype(F32)
            return value

        def advance(self):
            if self.pending is None:
                (self.high_piece,) = self.order.take(self.high_piece)
            else:
                if self.high_piece is not None:
                    self.high_piece = None
                    pending, self.low_piece = self.order.take(self.pending, self.low_piece)
                else:
                    (pending,) = self.order.take(self.pending)
                self.received.append(pending)
            if self.bits:
                half = self.rows // 2
                send = self.part(half, self.rows).astype(BF16)
                self.rows = half
                self.order.mark(send)
                self.pending = swap(send, self.bits.pop(0))
            else:
                self.result = self.part(0, self.rows)
                self.order.mark(self.result)

    def on_device(
        latents,
        timesteps,
        rel_index,
        time_table,
        rel_bias,
        w_mod,
        b_mod,
        w_qkv,
        w_time,
        w_out,
        b_out,
        w_up,
        b_up,
        w_down,
        b_down,
        cotangent,
    ):
        seq_len, model_width = latents.shape
        head_count, entries = rel_bias.shape
        hidden_count = b_up.shape[0]
        dp_at = lax.axis_index("dp")
        mp_at = lax.axis_index("mp")
        device = dp_at * mp_size + mp_at
        share = model_width // all_size

        peer_cotangent = swap(cotangent, 0)
        dp_blocks = relative_blocks([b - 1 for b in dp_order], dp_size)
        dp_source = source_columns(dp_blocks, dp_at, model_width)
        all_blocks = relative_blocks(all_order, all_size)
        all_source = source_columns(all_blocks, device, model_width)

        embedding = lax.dynamic_slice(time_table, (timesteps[0], 0), (1, model_width))
        (turned_keep, turned_send, qkv, probs, middle, mlp_in, mod) = front(
            latents,
            rel_index,
            rel_bias,
            embedding,
            b_mod[None, :],
            w_mod,
            w_qkv,
            w_time,
            w_out,
            b_out[None, :],
            all_source,
        )
        peer_in = swap(mlp_in, 0)
        bias_up = b_up[None, :]
        (own_act, own_pre, own_back, own_sum, own_out, rows_turned, grads_turned) = feed_forward(
            mlp_in, cotangent, w_up, bias_up, w_down, dp_source, True, (peer_cotangent,)
        )
        (peer_act, peer_pre, peer_back, peer_sum) = feed_forward(
            peer_in, peer_cotangent, w_up, bias_up, w_down, dp_source, False, (own_back,)
        )
        (turned_send,) = gate((turned_send,), (own_back,))
        turned_received = swap(turned_send, 0)
        back_received = swap(peer_back, 0)
        (down_high, down_low, down_keep, up_high, up_low, up_keep) = weight_products(
            peer_in,
            peer_cotangent,
            dp_source,
            rows_turned,
            grads_turned,
            own_act,
            peer_act,
            own_pre,
            peer_pre,
        )
        down_high, down_low, up_high, up_low = gate(
            (down_high, down_low, up_high, up_low), (back_received,)
        )
        order = Sequence()
        down = Halving(order, down_high, down_low, down_keep)
        up = Halving(order, up_high, up_low, up_keep)
        down.advance()
        up.advance()
        peer_out = forward_sum(peer_act, w_down, order.last)
        out_received = swap(peer_out, 0)

        (grad_middle, branch, grad_attended, sums, small) = branch_back(
            own_back,
            back_received,
            cotangent,
            middle,
            mod,
            w_out,
            own_sum,
            peer_sum,
            mp_at[None].astype(jnp.int32),
            (peer_out,),
        )
        peer_branch = swap(branch, 0)
        cut = 13 * model_width // 9
        (projected, proj_one, proj_two, late_sums, packed) = attention_back(
            grad_attended, qkv, probs, small, cut, (turned_received,)
        )
        peer_one = swap(proj_one, 0)
        peer_two = swap(proj_two, 0)
        order.mark(packed)
        (peer_branch,) = order.take(peer_branch)
        order.mark(peer_branch)
        down.advance()
        (grad_latents, images) = latents_back(
            projected,
            w_qkv,
            latents,
            mod,
            grad_middle,
            sums,
            late_sums,
            timesteps,
            order.last,
        )
        order.mark(images)

        message = first_message(packed, images, order.last)
        hop_bits = [dp_bits, dp_bits - 1, 0] + rest_bits[:-2] + [core]
        pending = swap(message, hop_bits.pop(0))

        def hop(packed, message, pending):
            (received,) = order.take(pending)
            packed, message = next_message(packed, message, received, ())
            order.mark(message)
            return packed, message, swap(message, hop_bits.pop(0))

        up.advance()
        high, low, keep = projection_products(
            turned_keep,
            turned_received,
            (branch, peer_branch),
            (proj_one, peer_one),
            "first_products",
            order.last,
        )
        order.mark(keep)
        one = Halving(order, high, low, keep)
        down.advance()
        packed, message, pending = hop(packed, message, pending)
        up.advance()
        one.advance()
        high, low, keep = projection_products(
            turned_keep,
            turned_received,
            None,
            (proj_two, peer_two),
            "second_products",
            order.last,
        )
        order.mark(keep)
        two = Halving(order, high, low, keep)
        down.advance()
        packed, message, pending = hop(packed, message, pending)
        up.advance()
        two.advance()
        one.advance()
        packed, message, pending = hop(packed, message, pending)
        two.advance()
        one.advance()
        packed, message, pending = hop(packed, message, pending)
        two.advance()
        while hop_bits:
            packed, message, pending = hop(packed, message, pending)
        (received,) = order.take(pending)
        own_w_mod = lax.dynamic_slice(w_mod, (device * share, 0), (share, 4 * model_width))
        own_w_time = lax.dynamic_slice(w_time, (device * share, 0), (share, 2 * model_width))
        (grad_rel_bias, grad_w_mod, grad_b_mod, grad_w_time, grad_table, lines) = small_gradients(
            packed,
            message,
            received,
            rel_index,
            time_table,
            own_w_mod,
            own_w_time,
            device[None].astype(jnp.int32),
            head_count,
            entries,
            all_size,
            mp_size,
            (),
        )
        order.mark(lines)
        grad_b_mod = grad_b_mod[0]
        while any(chain.result is None for chain in (down, up, one, two)):
            for chain in (down, up, one, two):
                if chain.result is None:
                    chain.advance()
        grad_w_down = down.result.T
        grad_w_up = up.result
        grad_w_out = one.result[:, :model_width]
        grad_w_qkv = jnp.concatenate([one.result[:, model_width:], two.result], axis=1)

        out = (
            middle + (own_out + out_received.astype(F32)) + b_down.astype(F32)[None, :]
        ).astype(BF16)

        line = lines.reshape(-1)
        grad_b_up = lax.dynamic_slice(line, (mp_at * hidden_count,), (hidden_count,))
        base = mp_size * hidden_count
        grad_b_out = lax.dynamic_slice(line, (base + device * share,), (share,))
        grad_b_down = lax.dynamic_slice(line, (base + model_width + device * share,), (share,))
        return (
            out,
            grad_latents,
            grad_table,
            grad_rel_bias,
            grad_w_mod,
            grad_b_mod,
            grad_w_qkv,
            grad_w_time,
            grad_w_out,
            grad_b_out,
            grad_w_up,
            grad_b_up,
            grad_w_down,
            grad_b_down,
        )

    return on_device


def solution(mesh):
    both = ("dp", "mp")
    in_specs = (
        P(both, None),
        P(both),
        P(),
        P(),
        P(),
        P(),
        P(),
        P(),
        P(),
        P(),
        P(),
        P(None, "mp"),
        P("mp"),
        P("mp", None),
        P(),
        P(both, None),
    )
    out_specs = (
        P(both, None),
        P(both, None),
        P(None, both),
        P(),
        P(both, None),
        P(both),
        P(both, None),
        P(both, None),
        P(both, None),
        P(both),
        P("dp", "mp"),
        P("mp"),
        P("mp", "dp"),
        P(both),
    )
    return jax.shard_map(
        make_device(mesh), mesh=mesh, in_specs=in_specs, out_specs=out_specs, check_vma=False
    )
```
